32 devices in a mesh: grp: 2 (over x), row: 16 (over z, y, core).
Axes of the slice: x: 2, y: 2, z: 4, core: 2. Of those that a mesh axis runs over, the one named last changes fastest.
Arguments:
- features: bfloat16 [16384, 128], P(('grp', 'row')), parts along dimension 0, may hold values from -6 to 6
- patterns: int32 [4096, 128, 128], P(('grp', 'row')), parts along dimension 0, may hold values 0 or 1
- tile_dest: int32 [4096, 1], P(('grp', 'row')), parts along dimension 0, may hold values from 0 to 15; in each aligned block of 128 rows (0 to 127, 128 to 255, ...) at most 9 rows name the same one
- tile_src_block: int32 [4096], P(('grp', 'row')), parts along dimension 0, may hold values from 0 to 3
- tile_dst_block: int32 [4096], P(('grp', 'row')), parts along dimension 0, may hold values from 0 to 3
- in_degree: int32 [16384], P(('grp', 'row')), parts along dimension 0, may hold values from 32 to 96
- w_self: bfloat16 [128, 256], replicated, may hold values from -0.5 to 0.5
- w_neigh: bfloat16 [128, 256], replicated, may hold values from -0.5 to 0.5
- bias: float32 [256], replicated, may hold values from -3 to 3
- cotangent: bfloat16 [16384, 256], P(('grp', 'row')), parts along dimension 0, may hold values from -6 to 6
Outputs:
- output: bfloat16 [16384, 256], P(('grp', 'row')), parts along dimension 0
- grad_feat: bfloat16 [16384, 128], P(('grp', 'row')), parts along dimension 0
- grad_self: float32 [256, 256], P('grp'), parts along dimension 0
- grad_neigh: float32 [256, 256], P('grp'), parts along dimension 0
- grad_bias: float32 [512], P('grp'), parts along dimension 0
The draws below stay inside these ranges and needn't reach their ends.
There are 2 independent parts, one for each index of `grp`. The reference program is written for one: setup_inputs(seed, part) draws one part's arguments, and reference() takes and returns one part's arrays. A program takes and returns all parts, laid end to end along the dimension named above; an argument that names none is the same for every part. Nothing has to cross between parts.
Inputs may be any that keep to these rules, and one draw needn't show every extreme that they name: `tile_dest`: among the 128 tiles of one device at most 9 have their destination on any one device, and in some devices exactly 9 share one destination device.
All inputs are finite; a program needn't handle non-finite values. No bound on the sum of `patterns` on one device may be relied on, other than what follows from the above.
Results may differ from the reference program's by a relative error of at most 0.0055.
The reference program's roundings to bfloat16 on the way count: a program that leaves them out, or rounds other values in their place, can miss the bound.
Values may be sent and summed in bfloat16 or wider, within the bound.
No kernel may reach another device: no remote copies, remote signals or barrier semaphores. Data moves between devices by JAX's collectives and lax.ppermute only.
A program may use at most 128 MiB of HBM per device.

```python
import math
import jax
import jax.numpy as jnp
import numpy as np
from jax import lax

F = 128
H = 256
TILE = 128
BLK_DEV = 4
TILES_DEV = 128
MOST = 9
VERTS = 8192
BLOCKS = 64
TILES = 2048
N_ROW = 16


def plant(values, stream_key, low, high):
    place = [jax.random.randint(jax.random.fold_in(stream_key, axis), (), 0, length) for axis, length in enumerate(values.shape)]
    widest = values.shape.index(max(values.shape))
    beside = place[:widest] + [(place[widest] + 1) % values.shape[widest]] + place[widest + 1:]
    return values.at[tuple(place)].set(low).at[tuple(beside)].set(high)


def block_levels(rng, dims, pieces, smallest, top_value):
    gain = 1.0
    for position, shards_of in pieces:
        heights = jax.random.uniform(jax.random.fold_in(jax.random.fold_in(rng, 6), position), (shards_of,), jnp.float32, smallest / len(pieces), top_value / len(pieces))
        gain = gain * jnp.repeat(jnp.exp(heights), dims[position] // shards_of).reshape((-1,) + (1,) * (len(dims) - 1 - position))
    return gain


def deal_out(own_key, own, number, rows, amount, top, bound, slope):
    sequence = jax.random.permutation(own_key, amount)
    heavy_load, usual = shares(amount, rows * top, bound, slope, True), shares(amount, rows * top, bound, slope, False)
    places = jnp.arange(amount)

    def named(sizes, offset_by):
        used = int((sizes > 0).sum())
        fixed = max(1, used // 4)
        moved = fixed + (places - fixed + offset_by * (used - fixed)) % max(1, amount - fixed)
        return jnp.zeros((amount,), jnp.int32).at[sequence[jnp.where(places < fixed, places, moved)]].set(jnp.asarray(sizes, jnp.int32))

    sizes = jnp.where(number % 4 == 0, named(heavy_load, number // 4), named(usual, number - number // 4 - 1))
    mixed = jax.random.permutation(jax.random.fold_in(own, 3), amount)
    source_of, receiver = mixed[0:amount // 2 * 2:2], mixed[1:amount // 2 * 2:2]
    slack = jnp.minimum(sizes[source_of] - 1, bound - sizes[receiver]) // 2
    slack = jnp.where((source_of == sequence[0]) | (receiver == sequence[0]) | (sizes[receiver] == 0), 0, jnp.maximum(slack, 0))
    moved = jax.random.randint(jax.random.fold_in(own, 4), (amount // 2,), 0, 1 << 20) % (slack + 1)
    sizes = sizes.at[source_of].add(-moved).at[receiver].add(moved)
    items = jnp.searchsorted(jnp.cumsum(sizes), jnp.arange(rows * top), side="right").astype(jnp.int32)
    table = items.reshape(top, rows).T
    table = table[jax.random.permutation(jax.random.fold_in(own, 1), rows)]
    offset_by = jax.random.randint(jax.random.fold_in(own, 2), (rows, 1), 0, top)
    return jnp.take_along_axis(table, (jnp.arange(top)[None, :] + offset_by) % top, axis=1)


def shares(number_of, total, limit, skew, full):
    weights = [(1 << 20) // math.isqrt(standing ** skew) + 1 for standing in range(1, number_of + 1)]
    largest = limit if full else min(limit, max(-(-total // number_of), total * weights[0] // sum(weights)))
    least = 1 if total - largest >= number_of - 1 else 0
    holding, rest = [largest] + [least] * (number_of - 1), total - largest - least * (number_of - 1)
    while rest > 0:
        candidates = [i for i in range(1, number_of) if holding[i] < largest] or [i for i in range(1, number_of) if holding[i] < limit]
        pool, budget = sum([weights[i] for i in candidates]), rest
        for i in candidates:
            more = min(limit - holding[i], max(1, budget * weights[i] // pool), rest)
            holding[i] = holding[i] + more
            rest = rest - more
    return np.array(holding)


def normal_values(key, shape, deviation, limit, split=(), held_as=jnp.bfloat16):
    drawn = jax.random.normal(key, shape, jnp.float32) * deviation
    if len(split) > 0:
        drawn = block_levels(key, shape, split, -0.22, 0.18) * drawn
    return jnp.clip(drawn, min=-limit, max=limit).astype(held_as)


def setup_inputs(seed: int = 0, part: int = 0) -> dict:
    key_of = jax.random.split(jax.random.key(seed), 11)
    part_keys = jax.random.split(jax.random.fold_in(key_of[10], part), 11)
    features = normal_values(part_keys[0], (VERTS, F), 1.0, 6.0, ((0, 16),))
    patterns = plant((jax.random.randint(part_keys[1], (TILES, TILE, TILE), 0, max(2, TILE // 2)) < 1).astype(jnp.int32), jax.random.fold_in(part_keys[1], 1), 0, 1)
    tile_dest_keys = jax.random.split(jax.random.fold_in(part_keys[2], 1), TILES // TILES_DEV)
    tile_dest_turns = jax.random.permutation(jax.random.fold_in(part_keys[2], 3), TILES // TILES_DEV)
    tile_dest = jax.vmap(lambda own, number: deal_out(jax.random.fold_in(part_keys[2], 2), own, number, TILES_DEV, N_ROW, 1, MOST, 2))(tile_dest_keys, tile_dest_turns).reshape((TILES, 1))
    tile_src_block = plant(jax.random.randint(part_keys[3], (TILES,), 0, BLK_DEV), jax.random.fold_in(part_keys[3], 1), 0, BLK_DEV - 1).astype(jnp.int32)
    tile_dst_block = plant(jax.random.randint(part_keys[4], (TILES,), 0, BLK_DEV), jax.random.fold_in(part_keys[4], 1), 0, BLK_DEV - 1).astype(jnp.int32)
    in_degree = plant(jax.random.randint(part_keys[5], (VERTS,), 32, 97), jax.random.fold_in(part_keys[5], 1), 32, 96).astype(jnp.int32)
    w_self = normal_values(key_of[6], (F, H), F ** -0.5, 0.5)
    w_neigh = normal_values(key_of[7], (F, H), F ** -0.5, 0.5)
    bias = normal_values(key_of[8], (H,), 0.5, 3.0, (), jnp.float32)
    cotangent = normal_values(part_keys[9], (VERTS, H), 1.0, 6.0, ((0, 16),))
    return dict(features=features, patterns=patterns, tile_dest=tile_dest, tile_src_block=tile_src_block, tile_dst_block=tile_dst_block, in_degree=in_degree, w_self=w_self, w_neigh=w_neigh, bias=bias, cotangent=cotangent)


def reference(features, patterns, tile_dest, tile_src_block, tile_dst_block, in_degree, w_self, w_neigh, bias, cotangent):
    blocks = features.reshape(BLOCKS, TILE, F)
    owner_dev = (jnp.arange(TILES, dtype=jnp.int32) // TILES_DEV).astype(jnp.int32)
    src_index = (owner_dev * BLK_DEV + tile_src_block).astype(jnp.int32)
    dst_index = (tile_dest[:, 0] * BLK_DEV + tile_dst_block).astype(jnp.int32)
    pat_groups = patterns.reshape(N_ROW, TILES_DEV, TILE, TILE)
    src_groups = src_index.reshape(N_ROW, TILES_DEV)
    dst_groups = dst_index.reshape(N_ROW, TILES_DEV)

    def forward_step(accum, item):
        pat_part, src_part, dst_part = item
        matrix = pat_part.astype(jnp.float32)
        source = blocks[src_part].astype(jnp.float32)
        partial_value = jnp.einsum('tsd,tsf->tdf', matrix, source).astype(jnp.bfloat16)
        partial_value = lax.optimization_barrier(partial_value).astype(jnp.float32)
        return (accum.at[dst_part].add(partial_value), None)
    summed, _ = lax.scan(forward_step, jnp.zeros((BLOCKS, TILE, F), jnp.float32), (pat_groups, src_groups, dst_groups))
    degree = 1.0 + in_degree.astype(jnp.float32)
    aggregate = (summed.reshape(VERTS, F) / degree[:, None]).astype(jnp.bfloat16)
    preact = jnp.dot(features, w_self, preferred_element_type=jnp.float32) + jnp.dot(aggregate, w_neigh, preferred_element_type=jnp.float32) + bias
    sigma = jax.nn.sigmoid(preact)
    output = (preact * sigma).astype(jnp.bfloat16)
    delta = (cotangent.astype(jnp.float32) * sigma * (1.0 + preact * (1.0 - sigma))).astype(jnp.bfloat16)
    grad_scale = 1.0 / math.sqrt(VERTS)
    grad_self = jnp.dot(features.T, delta, preferred_element_type=jnp.float32) * grad_scale
    grad_neigh = jnp.dot(aggregate.T, delta, preferred_element_type=jnp.float32) * grad_scale
    grad_bias = lax.optimization_barrier(jnp.sum(delta.astype(jnp.float32), axis=0)) * grad_scale
    back_agg = (jnp.dot(delta, w_neigh.T, preferred_element_type=jnp.float32) / degree[:, None]).astype(jnp.bfloat16)
    back_blocks = back_agg.reshape(BLOCKS, TILE, F)

    def backward_step(accum, item):
        pat_part, src_part, dst_part = item
        matrix = pat_part.astype(jnp.float32)
        picked = back_blocks[dst_part].astype(jnp.float32)
        contrib = jnp.einsum('tsd,tdf->tsf', matrix, picked)
        return (accum.at[src_part].add(contrib), None)
    spread, _ = lax.scan(backward_step, jnp.zeros((BLOCKS, TILE, F), jnp.float32), (pat_groups, src_groups, dst_groups))
    grad_feat = (jnp.dot(delta, w_self.T, preferred_element_type=jnp.float32) + spread.reshape(VERTS, F)).astype(jnp.bfloat16)
    return (output, grad_feat, grad_self, grad_neigh, grad_bias)
```

```python
import functools
import math

import jax
import jax.numpy as jnp
from jax import lax
from jax.experimental import pallas as pl
from jax.experimental.pallas import tpu as pltpu
from jax.sharding import PartitionSpec as P

BF16 = jnp.bfloat16
F32 = jnp.float32
GROUP = 8
MIB = 1 << 20


def swap(value, bits, devices):
    return lax.ppermute(value, "row", [(i, i ^ bits) for i in range(devices)])


def forward_kernel(
    parity, nb, group, slot_ref, x_ref, pat_hbm, s_ref, a_hbm, buf, adj, sems, out_sem
):
    step = pl.program_id(0)
    tiles = slot_ref.shape[0]
    per_unit = nb * nb
    rows = x_ref.shape[0]

    def mine(t):
        slot = slot_ref[t]
        unit = slot // per_unit
        return (unit % 2 == parity) & (unit // (2 * group) == step), slot

    def fetch(t):
        return pltpu.make_async_copy(pat_hbm.at[t], buf.at[t], sems.at[t])

    def start(t, carry):
        hit, _ = mine(t)

        @pl.when(hit)
        def _():
            fetch(t).start()

        return carry

    lax.fori_loop(0, tiles, start, 0)
    xt = x_ref[...].T

    def clear(i, carry):
        adj[pl.ds(i * per_unit, per_unit)] = jnp.zeros((per_unit,) + adj.shape[1:], BF16)
        return carry

    lax.fori_loop(0, group, clear, 0)

    def add(t, carry):
        hit, slot = mine(t)

        @pl.when(hit)
        def _():
            fetch(t).wait()
            unit = slot // per_unit
            place = (unit // 2) % group * per_unit + slot % per_unit
            adj[place] += buf[t].astype(F32).astype(BF16)

        return carry

    lax.fori_loop(0, tiles, add, 0)
    out = pltpu.make_async_copy(
        adj, a_hbm.at[pl.ds(step * group * per_unit, group * per_unit)], out_sem
    )
    out.start()
    tile = adj.shape[1]
    width = 2 if nb % 2 == 0 else 1

    def multiply(m, carry):
        for k in range(0, nb, width):
            weight = jnp.concatenate(
                [
                    adj[pl.ds((m * nb + k + j) * nb, nb)].reshape(rows, tile)
                    for j in range(width)
                ],
                axis=1,
            )
            s_ref[m, :, k * tile : (k + width) * tile] = jnp.dot(
                xt, weight, preferred_element_type=F32
            ).astype(s_ref.dtype)
        return carry

    lax.fori_loop(0, group, multiply, 0)
    out.wait()


def forward_sums(parity, units, dtype, slot, features, patterns, nb):
    rows, feat = features.shape
    tiles, tile, _ = patterns.shape
    group = min(GROUP, units)
    per_unit = nb * nb
    kernel = functools.partial(forward_kernel, parity, nb, group)
    return pl.pallas_call(
        kernel,
        grid_spec=pltpu.PrefetchScalarGridSpec(
            num_scalar_prefetch=1,
            grid=(units // group,),
            in_specs=[
                pl.BlockSpec((rows, feat), lambda g, s: (0, 0)),
                pl.BlockSpec(memory_space=pl.ANY),
            ],
            out_specs=[
                pl.BlockSpec((group, feat, rows), lambda g, s: (g, 0, 0)),
                pl.BlockSpec(memory_space=pl.ANY),
            ],
            scratch_shapes=[
                pltpu.VMEM((tiles, tile, tile), jnp.int32),
                pltpu.VMEM((group * per_unit, tile, tile), BF16),
                pltpu.SemaphoreType.DMA((tiles,)),
                pltpu.SemaphoreType.DMA,
            ],
        ),
        out_shape=[
            jax.ShapeDtypeStruct((units, feat, rows), dtype),
            jax.ShapeDtypeStruct((units * per_unit, tile, tile), BF16),
        ],
        compiler_params=pltpu.CompilerParams(vmem_limit_bytes=40 * MIB),
        cost_estimate=pl.CostEstimate(
            flops=2 * feat * rows * rows * units,
            bytes_accessed=tiles * tile * tile * 2 + units * rows * rows * 2,
            transcendentals=0,
        ),
        name="forward_sums",
    )(slot, features, patterns)


def layer_kernel(
    n_recv,
    own_ref,
    *refs,
):
    recv = refs[:n_recv]
    (deg_ref, x_ref, cot_ref, ws_ref, wn_ref, bias_ref) = refs[n_recv : n_recv + 6]
    out_ref, delta_ref, aggt_ref, back_ref = refs[n_recv + 6 :]
    total = own_ref[0].astype(F32)
    for r in recv:
        total += r[...].reshape(total.shape).astype(F32)
    degree = 1.0 + deg_ref[...].astype(F32)
    degree = jnp.broadcast_to(degree, total.shape)
    aggt = (total / degree).astype(BF16)
    aggt_ref[...] = aggt
    agg = aggt.T
    pre = (
        jnp.dot(x_ref[...], ws_ref[...], preferred_element_type=F32)
        + jnp.dot(agg, wn_ref[...], preferred_element_type=F32)
        + bias_ref[...]
    )
    sigma = jax.nn.sigmoid(pre)
    out_ref[...] = (pre * sigma).astype(BF16)
    delta = (cot_ref[...].astype(F32) * sigma * (1.0 + pre * (1.0 - sigma))).astype(BF16)
    delta_ref[...] = delta
    back = lax.dot_general(
        delta, wn_ref[...], (((1,), (1,)), ((), ())), preferred_element_type=F32
    )
    back_ref[...] = (back / degree.T).astype(BF16)


def layer(own, recv, in_degree, features, cotangent, w_self, w_neigh, bias):
    rows, feat = features.shape
    hidden = w_self.shape[1]

    def first(a):
        return pl.BlockSpec((1,) + a.shape[1:], lambda i: (0, 0, 0))

    def whole(a):
        return pl.BlockSpec(a.shape, lambda i, n=a.ndim: (0,) * n)

    rest = [in_degree, features, cotangent, w_self, w_neigh, bias]
    return pl.pallas_call(
        functools.partial(layer_kernel, len(recv)),
        grid=(1,),
        in_specs=[first(own)] + [first(r) for r in recv] + [whole(a) for a in rest],
        out_specs=[
            pl.BlockSpec((rows, hidden), lambda i: (0, 0)),
            pl.BlockSpec((rows, hidden), lambda i: (0, 0)),
            pl.BlockSpec((feat, rows), lambda i: (0, 0)),
            pl.BlockSpec((rows, feat), lambda i: (0, 0)),
        ],
        out_shape=[
            jax.ShapeDtypeStruct((rows, hidden), BF16),
            jax.ShapeDtypeStruct((rows, hidden), BF16),
            jax.ShapeDtypeStruct((feat, rows), BF16),
            jax.ShapeDtypeStruct((rows, feat), BF16),
        ],
        compiler_params=pltpu.CompilerParams(vmem_limit_bytes=24 * MIB),
        cost_estimate=pl.CostEstimate(
            flops=6 * rows * feat * hidden,
            bytes_accessed=4 * rows * hidden * 2,
            transcendentals=rows * hidden,
        ),
        name="layer",
    )(own, *recv, *rest)


def grad_kernel(scale, me_ref, x_ref, delta_ref, aggt_ref, ws_ref, g_ref, base_ref):
    delta = delta_ref[...]
    feat = x_ref.shape[1]
    gs = jnp.dot(x_ref[...].T, delta, preferred_element_type=F32) * scale
    gn = jnp.dot(aggt_ref[...], delta, preferred_element_type=F32) * scale
    gb = jnp.sum(delta.astype(F32), axis=0, keepdims=True) * scale
    gb = jnp.broadcast_to(gb, (8, gb.shape[1]))
    core = me_ref[0] % 2
    half = feat // 2
    for h in range(2):
        place = core ^ h
        g_ref[place, 0:half] = gs[h * half : (h + 1) * half]
        g_ref[place, half:feat] = gn[h * half : (h + 1) * half]
        g_ref[place, feat : feat + 8] = gb
    base_ref[...] = lax.dot_general(
        delta, ws_ref[...], (((1,), (1,)), ((), ())), preferred_element_type=F32
    )


def grad_terms(scale, me, features, delta, aggt, w_self):
    rows, feat = features.shape
    hidden = delta.shape[1]
    vm = pl.BlockSpec(memory_space=pltpu.VMEM)
    return pl.pallas_call(
        functools.partial(grad_kernel, scale),
        in_specs=[pl.BlockSpec(memory_space=pltpu.SMEM), vm, vm, vm, vm],
        out_specs=[vm, vm],
        out_shape=[
            jax.ShapeDtypeStruct((2, feat + 8, hidden), F32),
            jax.ShapeDtypeStruct((rows, feat), F32),
        ],
        compiler_params=pltpu.CompilerParams(vmem_limit_bytes=24 * MIB),
        cost_estimate=pl.CostEstimate(
            flops=6 * rows * feat * hidden, bytes_accessed=rows * hidden * 8, transcendentals=0
        ),
        name="grad_terms",
    )(me, features, delta, aggt, w_self)


def spread_kernel(places, nb, n_arrays, last, acc_ref, adj_hbm, *refs):
    backs = refs[:n_arrays]
    out_ref, adj, sems = refs[n_arrays:]
    per_unit = nb * nb
    copies = []
    for i, place in enumerate(places):
        copy = pltpu.make_async_copy(
            adj_hbm.at[pl.ds(place * per_unit, per_unit)], adj.at[i], sems.at[i]
        )
        copy.start()
        copies.append(copy)
    total = acc_ref[...]
    rows = total.shape[0]
    i = 0
    for back in backs:
        for j in range(back.shape[0]):
            copies[i].wait()
            tile = adj.shape[2]
            left = jnp.concatenate(
                [adj[i, k * nb : (k + 1) * nb].reshape(rows, tile) for k in range(nb)], axis=1
            )
            total += jnp.dot(left, back[j], preferred_element_type=F32)
            i += 1
    out_ref[...] = total.astype(out_ref.dtype)


def spread(acc, adjacency, places, backs, nb, dtype):
    vm = pl.BlockSpec(memory_space=pltpu.VMEM)
    rows, feat = acc.shape
    per_unit = nb * nb
    tile = adjacency.shape[1]
    n = len(places)
    return pl.pallas_call(
        functools.partial(spread_kernel, tuple(places), nb, len(backs), dtype != F32),
        in_specs=[vm, pl.BlockSpec(memory_space=pl.ANY)] + [vm] * len(backs),
        out_specs=vm,
        out_shape=jax.ShapeDtypeStruct((rows, feat), dtype),
        scratch_shapes=[
            pltpu.VMEM((n, per_unit, tile, tile), BF16),
            pltpu.SemaphoreType.DMA((n,)),
        ],
        compiler_params=pltpu.CompilerParams(vmem_limit_bytes=24 * MIB),
        cost_estimate=pl.CostEstimate(
            flops=2 * rows * rows * feat * n, bytes_accessed=rows * rows * 2 * n, transcendentals=0
        ),
        name="spread",
    )(acc, adjacency, *backs)


def stages_of(devices):
    bits = devices.bit_length() - 1
    assert 1 << bits == devices and bits >= 3
    rest = bits - 1
    return rest // 2, rest - rest // 2


def on_device(
    features,
    patterns,
    tile_dest,
    tile_src_block,
    tile_dst_block,
    in_degree,
    w_self,
    w_neigh,
    bias,
    cotangent,
):
    devices = lax.axis_size("row")
    me = lax.axis_index("row")
    tile = patterns.shape[1]
    rows, feat = features.shape
    nb = rows // tile
    y_bits, z_bits = stages_of(devices)
    ny, nz = 1 << y_bits, 1 << z_bits
    units = devices // 2
    small = devices <= 16

    unit = jnp.bitwise_xor(tile_dest[:, 0], me)
    slot = (unit * nb + tile_dst_block) * nb + tile_src_block

    s_other, a_other = forward_sums(1, units, BF16, slot, features, patterns, nb)
    s_recv = swap(s_other, 1, devices)
    s_own, a_own = forward_sums(0, units, F32 if small else BF16, slot, features, patterns, nb)

    def chip_sum(m):
        return s_own[m].astype(F32) + s_recv[m].astype(F32)

    if small:
        y_recv = [None] * nz
        for n in reversed(range(nz)):
            y_recv[n] = [
                swap(chip_sum(n * ny + k).astype(BF16), 2 * k, devices) for k in range(1, ny)
            ]
    else:
        s5 = s_own.reshape(nz, ny, feat, rows)
        r5 = s_recv.reshape(nz, ny, feat, rows)
        got = [
            swap((s5[:, k].astype(F32) + r5[:, k].astype(F32)).astype(BF16), 2 * k, devices)
            for k in range(1, ny)
        ]
        y_recv = [[g[n] for g in got] for n in range(nz)]
    z_recv = []
    for n in reversed(range(1, nz)):
        total = chip_sum(n * ny)
        for r in y_recv[n]:
            total = total + r.astype(F32)
        z_recv.append(swap(total.astype(BF16), 2 * ny * n, devices))

    output, delta, aggt, back = layer(
        s_own,
        [s_recv] + [r[None] for r in y_recv[0]] + [r[None] for r in z_recv],
        in_degree.reshape(1, rows),
        features,
        cotangent,
        w_self,
        w_neigh,
        bias.reshape(1, -1),
    )

    have = {0: back}
    for n in range(1, nz):
        have[n * ny] = swap(back, 2 * ny * n, devices)
    for n in range(nz):
        for k in range(1, ny):
            have[n * ny + k] = swap(have[n * ny], 2 * k, devices)
    other = {m: swap(have[m], 1, devices) for m in have}

    scale = 1.0 / math.sqrt(rows * devices)
    terms, base = grad_terms(scale, me.reshape(1).astype(jnp.int32), features, delta, aggt, w_self)
    half = terms[0] + swap(terms[1], 1, devices)
    bit = 2
    while bit < devices:
        half = half + swap(half, bit, devices)
        bit *= 2
    second = swap(half, 1, devices)
    even = me % 2 == 0
    low, high = jnp.where(even, half, second), jnp.where(even, second, half)
    h = feat // 2
    grad_self = jnp.concatenate([low[:h], high[:h]], axis=0)
    grad_neigh = jnp.concatenate([low[h:feat], high[h:feat]], axis=0)
    grad_bias = low[feat]

    acc = base
    order = sorted(have, key=lambda m: (m != 0, m))
    for at in range(0, units, GROUP):
        places = order[at : at + GROUP]
        acc = spread(acc, a_own, places, [have[m][None] for m in places], nb, F32)
    for at in range(0, units, GROUP):
        places = order[at : at + GROUP]
        dtype = BF16 if at + GROUP >= units else F32
        acc = spread(acc, a_other, places, [other[m][None] for m in places], nb, dtype)
    return (output, acc, grad_self, grad_neigh, grad_bias)


def solution(mesh):
    return jax.shard_map(
        on_device,
        mesh=mesh,
        in_specs=(
            P(("grp", "row"), None),
            P(("grp", "row"), None, None),
            P(("grp", "row"), None),
            P(("grp", "row")),
            P(("grp", "row")),
            P(("grp", "row")),
            P(),
            P(),
            P(),
            P(("grp", "row"), None),
        ),
        out_specs=(
            P(("grp", "row"), None),
            P(("grp", "row"), None),
            P("grp", None),
            P("grp", None),
            P("grp"),
        ),
        check_vma=False,
    )
```

```python
import functools
import math

import jax
import jax.numpy as jnp
from jax import lax
from jax.experimental import pallas as pl
from jax.experimental.pallas import tpu as pltpu
from jax.sharding import PartitionSpec as P

BF16 = jnp.bfloat16
F32 = jnp.float32
GROUP = 8
CHUNKS = 8
MIB = 1 << 20
LIGHT = pl.CostEstimate(flops=0, bytes_accessed=0, transcendentals=0)
HEAVY = pl.CostEstimate(flops=20_000_000_000, bytes_accessed=0, transcendentals=0)


def swap(value, bits, devices):
    return lax.ppermute(value, "row", [(i, i ^ bits) for i in range(devices)])


def build(nb, group, split, dest_ref, src_ref, dst_ref, pat_hbm, buf, adj, sems):
    step = pl.program_id(0)
    tiles = dest_ref.shape[0]
    per_unit = nb * nb
    chunks = sems.shape[0]
    size = tiles // chunks
    me = lax.axis_index("row")

    def fetch(c):
        part = pl.ds(c * size, size)
        return pltpu.make_async_copy(pat_hbm.at[part], buf.at[part], sems.at[c])

    @pl.when(step == 0)
    def _():
        for c in range(chunks):
            fetch(c).start()

    def clear(i, carry):
        adj[pl.ds(i * per_unit, per_unit)] = jnp.zeros((per_unit,) + adj.shape[1:], BF16)
        return carry

    lax.fori_loop(0, group, clear, 0)
    for c in range(chunks):

        @pl.when(step == 0)
        def _(c=c):
            fetch(c).wait()

        def add(i, carry, c=c):
            t = c * size + i
            unit = dest_ref[t] ^ me
            place = ((unit - step * group) * nb + dst_ref[t]) * nb + src_ref[t]

            def store():
                adj[place] += buf[t].astype(F32).astype(BF16)

            if split:
                pl.when((place >= 0) & (place < group * per_unit))(store)
            else:
                store()
            return carry

        lax.fori_loop(0, size, add, 0)


def forward_kernel(
    nb, group, split, dest_ref, src_ref, dst_ref, x_hbm, pat_hbm, odd_ref, even_ref, *scratch
):
    x_vmem, buf, adj, sems, x_sem = scratch
    tile = adj.shape[1]
    rows = x_vmem.shape[0]

    copy = pltpu.make_async_copy(x_hbm, x_vmem, x_sem)
    copy.start()
    build(nb, group, split, dest_ref, src_ref, dst_ref, pat_hbm, buf, adj, sems)
    copy.wait()
    xt = x_vmem[...].T
    width = 2 if nb % 2 == 0 else 1
    for parity, out_ref in ((1, odd_ref), (0, even_ref)):

        def multiply(m, carry, parity=parity, out_ref=out_ref):
            for k in range(0, nb, width):
                weight = jnp.concatenate(
                    [
                        adj[pl.ds(((2 * m + parity) * nb + k + j) * nb, nb)].reshape(rows, tile)
                        for j in range(width)
                    ],
                    axis=1,
                )
                out_ref[m, :, k * tile : (k + width) * tile] = jnp.dot(
                    xt, weight, preferred_element_type=F32
                ).astype(out_ref.dtype)
            return carry

        lax.fori_loop(0, group // 2, multiply, 0, unroll=True)


def forward_sums(units, own_dtype, tiles_at, features, patterns, nb):
    rows, feat = features.shape
    tiles, tile, _ = patterns.shape
    group = min(2 * GROUP, units)
    any_space = pl.BlockSpec(memory_space=pl.ANY)
    block = pl.BlockSpec((group // 2, feat, rows), lambda g: (g, 0, 0))
    return pl.pallas_call(
        functools.partial(forward_kernel, nb, group, units > group),
        grid=(units // group,),
        in_specs=[pl.BlockSpec(memory_space=pltpu.SMEM)] * 3 + [any_space, any_space],
        out_specs=[block, block],
        scratch_shapes=[
            pltpu.VMEM((rows, feat), BF16),
            pltpu.VMEM((tiles, tile, tile), jnp.int32),
            pltpu.VMEM((group * nb * nb, tile, tile), BF16),
            pltpu.SemaphoreType.DMA((CHUNKS,)),
            pltpu.SemaphoreType.DMA,
        ],
        out_shape=[
            jax.ShapeDtypeStruct((units // 2, feat, rows), BF16),
            jax.ShapeDtypeStruct((units // 2, feat, rows), own_dtype),
        ],
        compiler_params=pltpu.CompilerParams(vmem_limit_bytes=55 * MIB),
        cost_estimate=LIGHT,
        name="forward_sums",
    )(*tiles_at, features, patterns)


def adjacency_kernel(
    nb, group, split, dest_ref, src_ref, dst_ref, pat_hbm, after_hbm, a_hbm, made_ref, *scratch
):
    buf, adj, sems, out_sem = scratch
    made_ref[...] = jnp.zeros(made_ref.shape, F32)
    build(nb, group, split, dest_ref, src_ref, dst_ref, pat_hbm, buf, adj, sems)
    size = group * nb * nb
    out = pltpu.make_async_copy(adj, a_hbm.at[pl.ds(pl.program_id(0) * size, size)], out_sem)
    out.start()
    out.wait()


def adjacency(units, tiles_at, patterns, nb, after):
    tiles, tile, _ = patterns.shape
    group = min(2 * GROUP, units)
    any_space = pl.BlockSpec(memory_space=pl.ANY)
    return pl.pallas_call(
        functools.partial(adjacency_kernel, nb, group, units > group),
        grid=(units // group,),
        in_specs=[pl.BlockSpec(memory_space=pltpu.SMEM)] * 3 + [any_space, any_space],
        out_specs=[any_space, pl.BlockSpec((8, 128), lambda g: (0, 0))],
        scratch_shapes=[
            pltpu.VMEM((tiles, tile, tile), jnp.int32),
            pltpu.VMEM((group * nb * nb, tile, tile), BF16),
            pltpu.SemaphoreType.DMA((CHUNKS,)),
            pltpu.SemaphoreType.DMA,
        ],
        out_shape=[
            jax.ShapeDtypeStruct((units * nb * nb, tile, tile), BF16),
            jax.ShapeDtypeStruct((8, 128), F32),
        ],
        compiler_params=pltpu.CompilerParams(vmem_limit_bytes=20 * MIB),
        cost_estimate=LIGHT,
        name="adjacency",
    )(*tiles_at, patterns, after)


def add_kernel(n, total_ref, *refs):
    total = total_ref[0].astype(F32)
    for r in refs[:n]:
        total += r[0].astype(F32)
    refs[-1][0] = total


def add_first(total, parts, after):
    block = (1,) + total.shape[1:]
    spec = pl.BlockSpec(block, lambda i: (0, 0, 0))
    return pl.pallas_call(
        functools.partial(add_kernel, len(parts)),
        grid=(1,),
        in_specs=[spec] * (1 + len(parts)) + [pl.BlockSpec(memory_space=pl.ANY)],
        out_specs=spec,
        out_shape=jax.ShapeDtypeStruct(block, F32),
        compiler_params=pltpu.CompilerParams(vmem_limit_bytes=8 * MIB),
        cost_estimate=HEAVY,
        name="add_first",
    )(total, *parts, after)


def layer_kernel(n_recv, own_ref, *refs):
    recv = refs[:n_recv]
    (deg_ref, x_ref, cot_ref, ws_ref, wn_ref, bias_ref) = refs[n_recv : n_recv + 6]
    out_ref, delta_ref, aggt_ref, back_ref = refs[n_recv + 6 :]
    total = own_ref[0].astype(F32)
    for r in recv:
        total += r[...].reshape(total.shape).astype(F32)
    degree = 1.0 + deg_ref[...].astype(F32)
    degree = jnp.broadcast_to(degree, total.shape)
    aggt = (total / degree).astype(BF16)
    aggt_ref[...] = aggt
    agg = aggt.T
    pre = (
        jnp.dot(x_ref[...], ws_ref[...], preferred_element_type=F32)
        + jnp.dot(agg, wn_ref[...], preferred_element_type=F32)
        + bias_ref[...]
    )
    sigma = jax.nn.sigmoid(pre)
    out_ref[...] = (pre * sigma).astype(BF16)
    delta = (cot_ref[...].astype(F32) * sigma * (1.0 + pre * (1.0 - sigma))).astype(BF16)
    delta_ref[...] = delta
    back = lax.dot_general(
        delta, wn_ref[...], (((1,), (1,)), ((), ())), preferred_element_type=F32
    )
    back_ref[...] = (back / degree.T).astype(BF16)


def layer(own, recv, in_degree, features, cotangent, w_self, w_neigh, bias):
    rows, feat = features.shape
    hidden = w_self.shape[1]

    def first(a):
        return pl.BlockSpec((1,) + a.shape[1:], lambda i: (0, 0, 0))

    def whole(a):
        return pl.BlockSpec(a.shape, lambda i, n=a.ndim: (0,) * n)

    rest = [in_degree, features, cotangent, w_self, w_neigh, bias]
    return pl.pallas_call(
        functools.partial(layer_kernel, len(recv)),
        grid=(1,),
        in_specs=[first(own)] + [first(r) for r in recv] + [whole(a) for a in rest],
        out_specs=[
            pl.BlockSpec((rows, hidden), lambda i: (0, 0)),
            pl.BlockSpec((rows, hidden), lambda i: (0, 0)),
            pl.BlockSpec((feat, rows), lambda i: (0, 0)),
            pl.BlockSpec((rows, feat), lambda i: (0, 0)),
        ],
        out_shape=[
            jax.ShapeDtypeStruct((rows, hidden), BF16),
            jax.ShapeDtypeStruct((rows, hidden), BF16),
            jax.ShapeDtypeStruct((feat, rows), BF16),
            jax.ShapeDtypeStruct((rows, feat), BF16),
        ],
        compiler_params=pltpu.CompilerParams(vmem_limit_bytes=8 * MIB),
        cost_estimate=LIGHT,
        name="layer",
    )(own, *recv, *rest)


def grad_kernel(scale, me_ref, x_ref, delta_ref, aggt_ref, ws_ref, g_ref, base_ref):
    delta = delta_ref[...]
    feat = x_ref.shape[1]
    gs = jnp.dot(x_ref[...].T, delta, preferred_element_type=F32) * scale
    gn = jnp.dot(aggt_ref[...], delta, preferred_element_type=F32) * scale
    gb = jnp.sum(delta.astype(F32), axis=0, keepdims=True) * scale
    gb = jnp.broadcast_to(gb, (8, gb.shape[1]))
    core = me_ref[0] % 2
    half = feat // 2
    for h in range(2):
        place = core ^ h
        g_ref[place, 0:half] = gs[h * half : (h + 1) * half]
        g_ref[place, half:feat] = gn[h * half : (h + 1) * half]
        g_ref[place, feat : feat + 8] = gb
    base_ref[...] = lax.dot_general(
        delta, ws_ref[...], (((1,), (1,)), ((), ())), preferred_element_type=F32
    )


def grad_terms(scale, me, features, delta, aggt, w_self):
    rows, feat = features.shape
    hidden = delta.shape[1]
    vm = pl.BlockSpec(memory_space=pltpu.VMEM)
    return pl.pallas_call(
        functools.partial(grad_kernel, scale),
        in_specs=[pl.BlockSpec(memory_space=pltpu.SMEM), vm, vm, vm, vm],
        out_specs=[vm, vm],
        out_shape=[
            jax.ShapeDtypeStruct((2, feat + 8, hidden), F32),
            jax.ShapeDtypeStruct((rows, feat), F32),
        ],
        compiler_params=pltpu.CompilerParams(vmem_limit_bytes=8 * MIB),
        cost_estimate=LIGHT,
        name="grad_terms",
    )(me, features, delta, aggt, w_self)


def spread_kernel(places, nb, n_arrays, acc_ref, adj_hbm, *refs):
    backs = refs[:n_arrays]
    out_ref, adj, sems = refs[n_arrays], *refs[-2:]
    per_unit = nb * nb
    copies = []
    for i, place in enumerate(places):
        copy = pltpu.make_async_copy(
            adj_hbm.at[pl.ds(place * per_unit, per_unit)], adj.at[i], sems.at[i]
        )
        copy.start()
        copies.append(copy)
    total = acc_ref[...]
    rows = total.shape[0]
    i = 0
    for back in backs:
        for j in range(back.shape[0]):
            copies[i].wait()
            tile = adj.shape[2]
            left = jnp.concatenate(
                [adj[i, k * nb : (k + 1) * nb].reshape(rows, tile) for k in range(nb)], axis=1
            )
            total += jnp.dot(left, back[j], preferred_element_type=F32)
            i += 1
    out_ref[...] = total.astype(out_ref.dtype)


def finish_kernel(me_ref, mine_ref, theirs_ref, gs_ref, gn_ref, gb_ref):
    feat = gs_ref.shape[0]
    half = feat // 2
    core = me_ref[0] % 2
    for other, ref in ((0, mine_ref), (1, theirs_ref)):
        at = pl.ds(pl.multiple_of((core ^ other) * half, half), half)
        gs_ref[at] = ref[0:half]
        gn_ref[at] = ref[half:feat]
    gb_ref[...] = mine_ref[feat : feat + 1]


def finish(me, mine, theirs):
    vm = pl.BlockSpec(memory_space=pltpu.VMEM)
    rows, hidden = mine.shape
    feat = rows - 8
    return pl.pallas_call(
        finish_kernel,
        in_specs=[pl.BlockSpec(memory_space=pltpu.SMEM), vm, vm],
        out_specs=[vm] * 3,
        out_shape=[
            jax.ShapeDtypeStruct((feat, hidden), F32),
            jax.ShapeDtypeStruct((feat, hidden), F32),
            jax.ShapeDtypeStruct((1, hidden), F32),
        ],
        compiler_params=pltpu.CompilerParams(vmem_limit_bytes=4 * MIB),
        cost_estimate=LIGHT,
        name="finish",
    )(me, mine, theirs)


def spread(acc, adjacency, places, backs, nb, dtype):
    vm = pl.BlockSpec(memory_space=pltpu.VMEM)
    rows, feat = acc.shape
    per_unit = nb * nb
    tile = adjacency.shape[1]
    n = len(places)
    return pl.pallas_call(
        functools.partial(spread_kernel, tuple(places), nb, len(backs)),
        in_specs=[vm, pl.BlockSpec(memory_space=pl.ANY)] + [vm] * len(backs),
        out_specs=vm,
        out_shape=jax.ShapeDtypeStruct((rows, feat), dtype),
        scratch_shapes=[
            pltpu.VMEM((n, per_unit, tile, tile), BF16),
            pltpu.SemaphoreType.DMA((n,)),
        ],
        compiler_params=pltpu.CompilerParams(vmem_limit_bytes=12 * MIB),
        cost_estimate=HEAVY,
        name="spread",
    )(acc, adjacency, *backs)


def tree_sum(values):
    while len(values) > 1:
        values = [values[i] + values[i + 1] for i in range(0, len(values), 2)]
    return values[0]


def stages_of(devices):
    bits = devices.bit_length() - 1
    assert 1 << bits == devices and bits >= 3
    rest = bits - 1
    return rest // 2, rest - rest // 2


def on_device(
    features,
    patterns,
    tile_dest,
    tile_src_block,
    tile_dst_block,
    in_degree,
    w_self,
    w_neigh,
    bias,
    cotangent,
):
    devices = lax.axis_size("row")
    me = lax.axis_index("row")
    tile = patterns.shape[1]
    rows, feat = features.shape
    nb = rows // tile
    y_bits, z_bits = stages_of(devices)
    ny, nz = 1 << y_bits, 1 << z_bits
    units = devices // 2
    small = devices == 16

    tiles_at = (tile_dest.reshape(-1), tile_src_block, tile_dst_block)

    s_other, s_own = forward_sums(devices, F32 if small else BF16, tiles_at, features, patterns, nb)
    s_recv = swap(s_other, 1, devices)

    def chip_sum(m):
        return s_own[m].astype(F32) + s_recv[m].astype(F32)

    if small:
        y_recv = [None] * nz
        sent = None
        for n in reversed(range(nz)):
            y_recv[n] = []
            for k in range(1, ny):
                own, recv = s_own[n * ny + k], s_recv[n * ny + k]
                if sent is not None:
                    own, recv, sent = lax.optimization_barrier((own, recv, sent))
                sent = (own.astype(F32) + recv.astype(F32)).astype(BF16)
                y_recv[n].append(swap(sent, 2 * k, devices))
    else:
        s5 = s_own.reshape(nz, ny, feat, rows)
        r5 = s_recv.reshape(nz, ny, feat, rows)
        got = [
            swap((s5[:, k].astype(F32) + r5[:, k].astype(F32)).astype(BF16), 2 * k, devices)
            for k in range(1, ny)
        ]
        y_recv = [[g[n] for g in got] for n in range(nz)]
    z_recv = {}
    sent = None
    for n in reversed(range(1, nz)):
        arrived = y_recv[n]
        if sent is not None:
            arrived, sent = lax.optimization_barrier((arrived, sent))
        total = chip_sum(n * ny)
        for r in arrived:
            total = total + r.astype(F32)
        sent = total.astype(BF16)
        z_recv[n] = swap(sent, 2 * ny * n, devices)[None]
    adj, made = adjacency(devices, tiles_at, patterns, nb, sent)
    total = add_first(s_own, [s_recv, z_recv[nz - 1]], made)
    for n in reversed(range(2, nz - 1)):
        total = add_first(total, [z_recv[n]], made)

    output, delta, aggt, back = layer(
        total,
        [r[None] for r in y_recv[0]] + [z_recv[1]],
        in_degree.reshape(1, rows),
        features,
        cotangent,
        w_self,
        w_neigh,
        bias.reshape(1, -1),
    )
    me = me.reshape(1).astype(jnp.int32)
    scale = 1.0 / math.sqrt(rows * devices)
    terms, base = grad_terms(scale, me, features, delta, aggt, w_self)

    have = {0: back}
    for n in reversed(range(1, nz)):
        have[n * ny] = swap(back, 2 * ny * n, devices)
    for n in range(nz):
        for k in range(1, ny):
            have[n * ny + k] = swap(have[n * ny], 2 * k, devices)
    if small:
        pairs = [(0, 1), (2, 3), (4, 6), (5, 7)]
    else:
        pairs = [(m,) for m in sorted(have)]
    own = {2 * m: have[m][None] for m in have}
    across = {
        tuple(2 * m + 1 for m in pair): swap(jnp.stack([have[m] for m in pair]), 1, devices)
        for pair in pairs
    }

    half = terms[0] + swap(terms[1], 1, devices)
    half = tree_sum([half] + [swap(half, 2 * k, devices) for k in range(1, ny)])
    rounded = half.astype(BF16)
    half = tree_sum(
        [rounded.astype(F32)]
        + [swap(rounded, 2 * ny * n, devices).astype(F32) for n in range(1, nz)]
    )
    second = swap(half, 1, devices)

    if small:
        groups = [[0], [12, 8, 2, 4], [6, (1, 3)], [14, 10, (5, 7), (9, 13)], [(11, 15)]]
    else:
        singles = list(own) + list(across)
        groups = [singles[at : at + GROUP] for at in range(0, devices, GROUP)]
    grad_feat = base
    for i, group in enumerate(groups):
        dtype = BF16 if i == len(groups) - 1 else F32
        parts = [((u,), own[u]) if u in own else (u, across[u]) for u in group]
        places = [u for us, _ in parts for u in us]
        grad_feat = spread(grad_feat, adj, places, [b for _, b in parts], nb, dtype)
    grad_self, grad_neigh, grad_bias = finish(me, half, second)
    return (output, grad_feat, grad_self, grad_neigh, grad_bias.reshape(-1))


def solution(mesh):
    return jax.shard_map(
        on_device,
        mesh=mesh,
        in_specs=(
            P(("grp", "row"), None),
            P(("grp", "row"), None, None),
            P(("grp", "row"), None),
            P(("grp", "row")),
            P(("grp", "row")),
            P(("grp", "row")),
            P(),
            P(),
            P(),
            P(("grp", "row"), None),
        ),
        out_specs=(
            P(("grp", "row"), None),
            P(("grp", "row"), None),
            P("grp", None),
            P("grp", None),
            P("grp"),
        ),
        check_vma=False,
    )
```

```python
import functools
import math

import jax
import jax.numpy as jnp
from jax import lax
from jax.experimental import pallas as pl
from jax.experimental.pallas import tpu as pltpu
from jax.sharding import PartitionSpec as P

BF16 = jnp.bfloat16
F32 = jnp.float32
GROUP = 8
CHUNKS = 8
MIB = 1 << 20
ADJ_LIMIT = 38
PLAN = {'z': (1, 3, 2), 'y': (3, 2, 1, 0), 'parts': (), 'token': 0, 'after': 4, 'adj': 1, 'ysep': 1, 'agz': (3, 2, 1), 'groups': ((0,), (12, 4, 2, 8), (6, (1,), (3,), (5,)), (14, 10, (13,), (9,), (7,)), ((15,), (11,))), 'heavy': (1, 1, 1, 1, 1), 'pairs': ((0,), (2,), (4,), (6,), (8,), (12,), (10,), (14,)), 'terms': None, 'gy': None, 'gz': None, 'butter': 0, 'fin': 1, 'ph': 0, 'findep': 0, 'gyb': 1, 'direct': (1,), 'yfs': 0, 'agd': (1,), 'dsep': 0}
LIGHT = pl.CostEstimate(flops=0, bytes_accessed=0, transcendentals=0)
HEAVY = pl.CostEstimate(flops=20_000_000_000, bytes_accessed=0, transcendentals=0)


def swap(value, bits, devices):
    return lax.ppermute(value, "row", [(i, i ^ bits) for i in range(devices)])


def build(nb, group, split, dest_ref, src_ref, dst_ref, pat_hbm, buf, adj, sems):
    step = pl.program_id(0)
    tiles = dest_ref.shape[0]
    per_unit = nb * nb
    chunks = sems.shape[0]
    size = tiles // chunks
    me = lax.axis_index("row")

    def fetch(c):
        part = pl.ds(c * size, size)
        return pltpu.make_async_copy(pat_hbm.at[part], buf.at[part], sems.at[c])

    @pl.when(step == 0)
    def _():
        for c in range(chunks):
            fetch(c).start()

    def clear(i, carry):
        adj[pl.ds(i * per_unit, per_unit)] = jnp.zeros((per_unit,) + adj.shape[1:], BF16)
        return carry

    lax.fori_loop(0, group, clear, 0)
    for c in range(chunks):

        @pl.when(step == 0)
        def _(c=c):
            fetch(c).wait()

        def add(i, carry, c=c):
            t = c * size + i
            unit = dest_ref[t] ^ me
            place = ((unit - step * group) * nb + dst_ref[t]) * nb + src_ref[t]

            def store():
                adj[place] += buf[t].astype(F32).astype(BF16)

            if split:
                pl.when((place >= 0) & (place < group * per_unit))(store)
            else:
                store()
            return carry

        lax.fori_loop(0, size, add, 0)


def forward_kernel(
    nb, group, split, dest_ref, src_ref, dst_ref, x_hbm, pat_hbm, odd_hbm, even_hbm, *scratch
):
    x_vmem, buf, adj, odd, even, sems, x_sem, out_sems = scratch
    tile = adj.shape[1]
    rows = x_vmem.shape[0]
    copy = pltpu.make_async_copy(x_hbm, x_vmem, x_sem)
    copy.start()
    build(nb, group, split, dest_ref, src_ref, dst_ref, pat_hbm, buf, adj, sems)
    copy.wait()
    xt = x_vmem[...].T
    width = 2 if nb % 2 == 0 else 1
    half = group // 2
    step = pl.program_id(0)
    outs = []
    for parity, sums, out_hbm in ((1, odd, odd_hbm), (0, even, even_hbm)):
        for m in range(half):
            for k in range(0, nb, width):
                weight = jnp.concatenate(
                    [
                        adj[pl.ds(((2 * m + parity) * nb + k + j) * nb, nb)].reshape(rows, tile)
                        for j in range(width)
                    ],
                    axis=1,
                )
                sums[m, :, k * tile : (k + width) * tile] = jnp.dot(
                    xt, weight, preferred_element_type=F32
                ).astype(sums.dtype)
            if m % 2 == 1 or m == half - 1:
                first = m - m % 2
                part = pl.ds(first, m + 1 - first)
                out = pltpu.make_async_copy(
                    sums.at[part],
                    out_hbm.at[pl.ds(step * half + first, m + 1 - first)],
                    out_sems.at[parity, m // 2],
                )
                out.start()
                outs.append(out)
    for out in outs:
        out.wait()


def forward_sums(units, own_dtype, tiles_at, features, patterns, nb):
    rows, feat = features.shape
    tiles, tile, _ = patterns.shape
    group = min(2 * GROUP, units)
    any_space = pl.BlockSpec(memory_space=pl.ANY)
    return pl.pallas_call(
        functools.partial(forward_kernel, nb, group, units > group),
        grid=(units // group,),
        in_specs=[pl.BlockSpec(memory_space=pltpu.SMEM)] * 3 + [any_space, any_space],
        out_specs=[any_space, any_space],
        scratch_shapes=[
            pltpu.VMEM((rows, feat), BF16),
            pltpu.VMEM((tiles, tile, tile), jnp.int32),
            pltpu.VMEM((group * nb * nb, tile, tile), BF16),
            pltpu.VMEM((group // 2, feat, rows), BF16),
            pltpu.VMEM((group // 2, feat, rows), own_dtype),
            pltpu.SemaphoreType.DMA((CHUNKS,)),
            pltpu.SemaphoreType.DMA,
            pltpu.SemaphoreType.DMA((2, -(-group // 4))),
        ],
        out_shape=[
            jax.ShapeDtypeStruct((units // 2, feat, rows), BF16),
            jax.ShapeDtypeStruct((units // 2, feat, rows), own_dtype),
        ],
        compiler_params=pltpu.CompilerParams(vmem_limit_bytes=55 * MIB),
        cost_estimate=LIGHT,
        name="forward_sums",
    )(*tiles_at, features, patterns)


def adjacency_kernel(
    nb, group, split, dest_ref, src_ref, dst_ref, pat_hbm, after_hbm, adj, made_ref, *scratch
):
    buf, sems = scratch
    made_ref[...] = jnp.zeros(made_ref.shape, F32)
    build(nb, group, split, dest_ref, src_ref, dst_ref, pat_hbm, buf, adj, sems)


def adjacency(units, tiles_at, patterns, nb, after):
    tiles, tile, _ = patterns.shape
    group = min(2 * GROUP, units)
    any_space = pl.BlockSpec(memory_space=pl.ANY)
    blocks = group * nb * nb
    if units > group:
        out_spec = pl.BlockSpec((blocks, tile, tile), lambda g: (g, 0, 0))
    else:
        out_spec = pl.BlockSpec(memory_space=pltpu.VMEM)
    return pl.pallas_call(
        functools.partial(adjacency_kernel, nb, group, units > group),
        grid=(units // group,),
        in_specs=[pl.BlockSpec(memory_space=pltpu.SMEM)] * 3 + [any_space, any_space],
        out_specs=[out_spec, pl.BlockSpec((8, 128), lambda g: (0, 0))],
        scratch_shapes=[
            pltpu.VMEM((tiles, tile, tile), jnp.int32),
            pltpu.SemaphoreType.DMA((CHUNKS,)),
        ],
        out_shape=[
            jax.ShapeDtypeStruct((units * nb * nb, tile, tile), BF16),
            jax.ShapeDtypeStruct((8, 128), F32),
        ],
        compiler_params=pltpu.CompilerParams(vmem_limit_bytes=ADJ_LIMIT * MIB),
        cost_estimate=HEAVY if PLAN["adj"] else LIGHT,
        name="adjacency",
    )(*tiles_at, patterns, after)


def add_kernel(n, total_ref, *refs):
    total = total_ref[0].astype(F32)
    for r in refs[:n]:
        total += r[0].astype(F32)
    refs[-1][0] = total


def add_first(total, parts, after):
    block = (1,) + total.shape[1:]
    spec = pl.BlockSpec(block, lambda i: (0, 0, 0))
    return pl.pallas_call(
        functools.partial(add_kernel, len(parts)),
        grid=(1,),
        in_specs=[spec] * (1 + len(parts)) + [pl.BlockSpec(memory_space=pl.ANY)],
        out_specs=spec,
        out_shape=jax.ShapeDtypeStruct(block, F32),
        compiler_params=pltpu.CompilerParams(vmem_limit_bytes=8 * MIB),
        cost_estimate=HEAVY if PLAN["ph"] else LIGHT,
        name="add_first",
    )(total, *parts, after)


def layer_kernel(n_recv, own_ref, *refs):
    recv = refs[:n_recv]
    (deg_ref, x_ref, cot_ref, ws_ref, wn_ref, bias_ref) = refs[n_recv : n_recv + 6]
    out_ref, delta_ref, aggt_ref, back_ref = refs[n_recv + 6 :]
    total = own_ref[0].astype(F32)
    for r in recv:
        total += r[...].reshape(total.shape).astype(F32)
    degree = 1.0 + deg_ref[...].astype(F32)
    degree = jnp.broadcast_to(degree, total.shape)
    aggt = (total / degree).astype(BF16)
    aggt_ref[...] = aggt
    agg = aggt.T
    pre = (
        jnp.dot(x_ref[...], ws_ref[...], preferred_element_type=F32)
        + jnp.dot(agg, wn_ref[...], preferred_element_type=F32)
        + bias_ref[...]
    )
    sigma = jax.nn.sigmoid(pre)
    out_ref[...] = (pre * sigma).astype(BF16)
    delta = (cot_ref[...].astype(F32) * sigma * (1.0 + pre * (1.0 - sigma))).astype(BF16)
    delta_ref[...] = delta
    back = lax.dot_general(
        delta, wn_ref[...], (((1,), (1,)), ((), ())), preferred_element_type=F32
    )
    back_ref[...] = (back / degree.T).astype(BF16)


def layer(own, recv, in_degree, features, cotangent, w_self, w_neigh, bias):
    rows, feat = features.shape
    hidden = w_self.shape[1]

    def first(a):
        return pl.BlockSpec((1,) + a.shape[1:], lambda i: (0, 0, 0))

    def whole(a):
        return pl.BlockSpec(a.shape, lambda i, n=a.ndim: (0,) * n)

    rest = [in_degree, features, cotangent, w_self, w_neigh, bias]
    return pl.pallas_call(
        functools.partial(layer_kernel, len(recv)),
        grid=(1,),
        in_specs=[first(own)] + [first(r) for r in recv] + [whole(a) for a in rest],
        out_specs=[
            pl.BlockSpec((rows, hidden), lambda i: (0, 0)),
            pl.BlockSpec((rows, hidden), lambda i: (0, 0)),
            pl.BlockSpec((feat, rows), lambda i: (0, 0)),
            pl.BlockSpec((rows, feat), lambda i: (0, 0)),
        ],
        out_shape=[
            jax.ShapeDtypeStruct((rows, hidden), BF16),
            jax.ShapeDtypeStruct((rows, hidden), BF16),
            jax.ShapeDtypeStruct((feat, rows), BF16),
            jax.ShapeDtypeStruct((rows, feat), BF16),
        ],
        compiler_params=pltpu.CompilerParams(vmem_limit_bytes=8 * MIB),
        cost_estimate=LIGHT,
        name="layer",
    )(own, *recv, *rest)


def grad_kernel(scale, me_ref, x_ref, delta_ref, aggt_ref, ws_ref, g_ref, base_ref):
    delta = delta_ref[...]
    feat = x_ref.shape[1]
    gs = jnp.dot(x_ref[...].T, delta, preferred_element_type=F32) * scale
    gn = jnp.dot(aggt_ref[...], delta, preferred_element_type=F32) * scale
    gb = jnp.sum(delta.astype(F32), axis=0, keepdims=True) * scale
    gb = jnp.broadcast_to(gb, (8, gb.shape[1]))
    core = me_ref[0] % 2
    half = feat // 2
    for h in range(2):
        place = core ^ h
        g_ref[place, 0:half] = gs[h * half : (h + 1) * half]
        g_ref[place, half:feat] = gn[h * half : (h + 1) * half]
        g_ref[place, feat : feat + 8] = gb
    base_ref[...] = lax.dot_general(
        delta, ws_ref[...], (((1,), (1,)), ((), ())), preferred_element_type=F32
    )


def grad_terms(scale, me, features, delta, aggt, w_self):
    rows, feat = features.shape
    hidden = delta.shape[1]
    vm = pl.BlockSpec(memory_space=pltpu.VMEM)
    return pl.pallas_call(
        functools.partial(grad_kernel, scale),
        in_specs=[pl.BlockSpec(memory_space=pltpu.SMEM), vm, vm, vm, vm],
        out_specs=[vm, vm],
        out_shape=[
            jax.ShapeDtypeStruct((2, feat + 8, hidden), F32),
            jax.ShapeDtypeStruct((rows, feat), F32),
        ],
        compiler_params=pltpu.CompilerParams(vmem_limit_bytes=8 * MIB),
        cost_estimate=LIGHT,
        name="grad_terms",
    )(me, features, delta, aggt, w_self)


def spread_kernel(places, nb, n_arrays, acc_ref, adj_hbm, *refs):
    backs = refs[:n_arrays]
    out_ref, adj, sems = refs[n_arrays], *refs[-2:]
    per_unit = nb * nb
    copies = []
    for i, place in enumerate(places):
        copy = pltpu.make_async_copy(
            adj_hbm.at[pl.ds(place * per_unit, per_unit)], adj.at[i], sems.at[i]
        )
        copy.start()
        copies.append(copy)
    total = acc_ref[...]
    rows = total.shape[0]
    i = 0
    for back in backs:
        for j in range(back.shape[0]):
            copies[i].wait()
            tile = adj.shape[2]
            left = jnp.concatenate(
                [adj[i, k * nb : (k + 1) * nb].reshape(rows, tile) for k in range(nb)], axis=1
            )
            total += jnp.dot(left, back[j], preferred_element_type=F32)
            i += 1
    out_ref[...] = total.astype(out_ref.dtype)


def finish_kernel(me_ref, mine_ref, theirs_ref, *refs):
    gs_ref, gn_ref, gb_ref = refs[-3:]
    feat = gs_ref.shape[0]
    half = feat // 2
    core = me_ref[0] % 2
    for other, ref in ((0, mine_ref), (1, theirs_ref)):
        at = pl.ds(pl.multiple_of((core ^ other) * half, half), half)
        gs_ref[at] = ref[0:half]
        gn_ref[at] = ref[half:feat]
    gb_ref[...] = mine_ref[feat : feat + 1]


def finish(me, mine, theirs, after):
    vm = pl.BlockSpec(memory_space=pltpu.VMEM)
    rows, hidden = mine.shape
    feat = rows - 8
    return pl.pallas_call(
        finish_kernel,
        in_specs=[pl.BlockSpec(memory_space=pltpu.SMEM), vm, vm]
        + [pl.BlockSpec(memory_space=pl.ANY)] * len(after),
        out_specs=[vm] * 3,
        out_shape=[
            jax.ShapeDtypeStruct((feat, hidden), F32),
            jax.ShapeDtypeStruct((feat, hidden), F32),
            jax.ShapeDtypeStruct((1, hidden), F32),
        ],
        compiler_params=pltpu.CompilerParams(vmem_limit_bytes=4 * MIB),
        cost_estimate=LIGHT,
        name="finish",
    )(me, mine, theirs, *after)


def last_kernel(places, nb, n_arrays, me_ref, mine_ref, theirs_ref, acc_ref, adj_hbm, *refs):
    backs, out_ref, grads, scratch = refs[:n_arrays], refs[n_arrays], refs[-5:-2], refs[-2:]
    finish_kernel(me_ref, mine_ref, theirs_ref, *grads)
    spread_kernel(places, nb, n_arrays, acc_ref, adj_hbm, *backs, out_ref, *scratch)


def spread(acc, adjacency, places, backs, nb, dtype, heavy=True, grads=None):
    vm = pl.BlockSpec(memory_space=pltpu.VMEM)
    rows, feat = acc.shape
    per_unit = nb * nb
    tile = adjacency.shape[1]
    n = len(places)
    in_specs = [vm, pl.BlockSpec(memory_space=pl.ANY)] + [vm] * len(backs)
    inputs = [acc, adjacency, *backs]
    kernel, out_shape = spread_kernel, jax.ShapeDtypeStruct((rows, feat), dtype)
    if grads is not None:
        in_specs = [pl.BlockSpec(memory_space=pltpu.SMEM), vm, vm] + in_specs
        inputs = [*grads, *inputs]
        hidden = grads[1].shape[1]
        kernel = last_kernel
        out_shape = [
            out_shape,
            jax.ShapeDtypeStruct((feat, hidden), F32),
            jax.ShapeDtypeStruct((feat, hidden), F32),
            jax.ShapeDtypeStruct((1, hidden), F32),
        ]
    return pl.pallas_call(
        functools.partial(kernel, tuple(places), nb, len(backs)),
        in_specs=in_specs,
        out_specs=jax.tree.map(lambda _: vm, out_shape),
        out_shape=out_shape,
        scratch_shapes=[
            pltpu.VMEM((n, per_unit, tile, tile), BF16),
            pltpu.SemaphoreType.DMA((n,)),
        ],
        compiler_params=pltpu.CompilerParams(vmem_limit_bytes=12 * MIB),
        cost_estimate=HEAVY if heavy else LIGHT,
        name="spread",
    )(*inputs)


def tree_sum(values):
    while len(values) > 1:
        values = [values[i] + values[i + 1] for i in range(0, len(values), 2)]
    return values[0]


def stages_of(devices):
    bits = devices.bit_length() - 1
    assert 1 << bits == devices and bits >= 3
    rest = bits - 1
    return rest // 2, rest - rest // 2


def on_device(
    features,
    patterns,
    tile_dest,
    tile_src_block,
    tile_dst_block,
    in_degree,
    w_self,
    w_neigh,
    bias,
    cotangent,
):
    devices = lax.axis_size("row")
    me = lax.axis_index("row")
    tile = patterns.shape[1]
    rows, feat = features.shape
    nb = rows // tile
    y_bits, z_bits = stages_of(devices)
    ny, nz = 1 << y_bits, 1 << z_bits
    units = devices // 2
    small = devices == 16

    tiles_at = (tile_dest.reshape(-1), tile_src_block, tile_dst_block)

    s_other, s_own = forward_sums(devices, F32 if small else BF16, tiles_at, features, patterns, nb)
    s_recv = swap(s_other, 1, devices)

    def chip_sum(m):
        return s_own[m].astype(F32) + s_recv[m].astype(F32)

    if small:
        y_recv = [None] * nz
        sent = None
        for n in PLAN["y"]:
            y_recv[n] = []
            if n in PLAN["direct"]:
                continue
            for k in range(1, ny):
                own, recv = s_own[n * ny + k], s_recv[n * ny + k]
                if sent is not None and PLAN["ysep"]:
                    own, recv, sent = lax.optimization_barrier((own, recv, sent))
                sent = (own.astype(F32) + recv.astype(F32)).astype(BF16)
                y_recv[n].append(swap(sent, 2 * k, devices))
    else:
        s5 = s_own.reshape(nz, ny, feat, rows)
        r5 = s_recv.reshape(nz, ny, feat, rows)
        got = [
            swap((s5[:, k].astype(F32) + r5[:, k].astype(F32)).astype(BF16), 2 * k, devices)
            for k in range(1, ny)
        ]
        y_recv = [[g[n] for g in got] for n in range(nz)]
    z_recv = {}
    sent = None
    sums, first_sent, sent = {}, sent if small else None, None
    for n in PLAN["z"] if small else reversed(range(1, nz)):
        arrived = y_recv[n]
        if small and n in PLAN["direct"]:
            for k in range(ny):
                m = n * ny + k
                mine, recv, sent = s_own[m], s_recv[m], first_sent
                if PLAN["dsep"]:
                    mine, recv, sent = lax.optimization_barrier((mine, recv, sent))
                direct = (mine.astype(F32) + recv.astype(F32)).astype(BF16)
                z_recv[m / ny] = swap(direct, 2 * m, devices)[None]
            continue
        if sent is not None:
            arrived, sent = lax.optimization_barrier((arrived, sent))
        total = chip_sum(n * ny)
        for r in arrived:
            total = total + r.astype(F32)
        sums[n] = sent = total.astype(BF16)
        z_recv[n] = swap(sent, 2 * ny * n, devices)[None]
    after = PLAN["after"] if small else 1
    made = s_recv
    if after == 4:
        adj, made = adjacency(devices, tiles_at, patterns, nb, z_recv[3])
        in_degree, made = lax.optimization_barrier((in_degree, made))
    elif after:
        adj, made = adjacency(devices, tiles_at, patterns, nb, sums[after])
    total, summed = s_own, ()
    parts = PLAN["parts"] if small else [(n,) for n in range(2, nz)]
    for i, part in enumerate(parts):
        extra = [s_recv] if i == 0 else []
        total = add_first(total, extra + [z_recv[n] for n in part], made)
        summed += part
    if not parts:
        summed = ()
    rest = [z_recv[n] for n in z_recv if n not in summed]

    output, delta, aggt, back = layer(
        total,
        ([s_recv] if not parts else []) + [r[None] for r in y_recv[0]] + rest,
        in_degree.reshape(1, rows),
        features,
        cotangent,
        w_self,
        w_neigh,
        bias.reshape(1, -1),
    )
    if not after:
        adj, made = adjacency(devices, tiles_at, patterns, nb, back)
    me = me.reshape(1).astype(jnp.int32)
    scale = 1.0 / math.sqrt(rows * devices)
    terms, base = grad_terms(scale, me, features, delta, aggt, w_self)

    have = {0: back}
    for n in PLAN["agz"] if small else range(1, nz):
        have[n * ny] = swap(back, 2 * ny * n, devices)
    own = {0: back[None]}
    onward = []
    for n in range(nz):
        own[2 * n * ny] = have[n * ny][None]
        for k in range(1, ny):
            m = n * ny + k
            if small and n in PLAN["agd"]:
                own[2 * m] = swap(back, 2 * m, devices)[None]
            elif small and PLAN["yfs"] and n > 0:
                onward.append(n)
            else:
                own[2 * m] = swap(have[n * ny], 2 * k, devices)[None]
    if onward:
        key = tuple(2 * n * ny + 2 for n in onward)
        own[key] = swap(jnp.stack([have[n * ny] for n in onward]), 2, devices)

    def plus_one(key):
        return tuple(u + 1 for u in key) if isinstance(key, tuple) else (key + 1,)

    across = {}
    for keys in PLAN["pairs"] if small else [(key,) for key in own]:
        name = sum((plus_one(key) for key in keys), ())
        parts = [own[key] for key in keys]
        whole = jnp.concatenate(parts, axis=0) if len(parts) > 1 else parts[0]
        across[name] = swap(whole, 1, devices)

    def later(value, what):
        key = PLAN[what]
        if key is None or not small:
            return value
        value, own[key] = lax.optimization_barrier((value, own[key]))
        return value

    terms = later(terms, "terms")
    half = terms[0] + swap(terms[1], 1, devices)
    half = later(half, "gy")
    if PLAN["gyb"]:
        half = half.astype(BF16)
    half = tree_sum(
        [half.astype(F32)] + [swap(half, 2 * k, devices).astype(F32) for k in range(1, ny)]
    )
    half = later(half, "gz")
    if PLAN["butter"] and small:
        for n in (1, 2):
            rounded = half.astype(BF16)
            half = rounded.astype(F32) + swap(rounded, 2 * ny * n, devices).astype(F32)
    else:
        rounded = half.astype(BF16)
        half = tree_sum(
            [rounded.astype(F32)]
            + [swap(rounded, 2 * ny * n, devices).astype(F32) for n in range(1, nz)]
        )
    second = swap(half, 1, devices)

    if small:
        groups, heavy = PLAN["groups"], PLAN["heavy"]
    else:
        singles = list(own) + list(across)
        groups = [singles[at : at + GROUP] for at in range(0, devices, GROUP)]
        heavy = [1] * len(groups)
    grad_feat = base
    for i, group in enumerate(groups):
        last = i == len(groups) - 1
        parts = [(u, own[u]) if u in own else (u, across[u]) for u in group]
        parts = [(u if isinstance(u, tuple) else (u,), b) for u, b in parts]
        places = [u for us, _ in parts for u in us]
        grad_feat = spread(
            grad_feat,
            adj,
            places,
            [b for _, b in parts],
            nb,
            BF16 if last else F32,
            heavy[i],
            (me, half, second) if last and PLAN["fin"] else None,
        )
    if PLAN["fin"]:
        grad_feat, grad_self, grad_neigh, grad_bias = grad_feat
    else:
        grad_self, grad_neigh, grad_bias = finish(me, half, second, [grad_feat] if PLAN["findep"] else [])
    return (output, grad_feat, grad_self, grad_neigh, grad_bias.reshape(-1))


def solution(mesh):
    return jax.shard_map(
        on_device,
        mesh=mesh,
        in_specs=(
            P(("grp", "row"), None),
            P(("grp", "row"), None, None),
            P(("grp", "row"), None),
            P(("grp", "row")),
            P(("grp", "row")),
            P(("grp", "row")),
            P(),
            P(),
            P(),
            P(("grp", "row"), None),
        ),
        out_specs=(
            P(("grp", "row"), None),
            P(("grp", "row"), None),
            P("grp", None),
            P("grp", None),
            P("grp"),
        ),
        check_vma=False,
    )
```

```python
import functools
import math

import jax
import jax.numpy as jnp
from jax import lax
from jax.experimental import pallas as pl
from jax.experimental.pallas import tpu as pltpu
from jax.sharding import PartitionSpec as P

BF16 = jnp.bfloat16
F32 = jnp.float32
GROUP = 8
CHUNKS = 8
MIB = 1 << 20
PLAN = {'z': (1, 3, 2), 'y': (3, 2, 1, 0), 'parts': (), 'token': 0, 'after': 4, 'adj': 1, 'ysep': 1, 'agz': (3, 2, 1), 'groups': ((0,), (12, 4, 2, 8, 6, (1,), (3,), (5,)), (14, 10, (13,), (9,), (7,)), ((15,), (11,))), 'heavy': (1, 1, 1, 1), 'pairs': ((0,), (2,), (4,), (6,), (8,), (12,), (10,), (14,)), 'terms': None, 'gy': None, 'gz': None, 'butter': 0, 'fin': 1, 'ph': 0, 'findep': 0, 'gyb': 1, 'direct': (1,), 'yfs': 0, 'agd': (1,), 'dsep': 0, 'k1l': 55, 'adjl': 38, 'gates': ((1, (12, 4, 2, 8), 1),), 'halves': ((7, 5, 2, 3), (0, 6, 4, 1))}
LIGHT = pl.CostEstimate(flops=0, bytes_accessed=0, transcendentals=0)
HEAVY = pl.CostEstimate(flops=20_000_000_000, bytes_accessed=0, transcendentals=0)


def swap(value, bits, devices):
    return lax.ppermute(value, "row", [(i, i ^ bits) for i in range(devices)])


def build(nb, group, split, dest_ref, src_ref, dst_ref, pat_hbm, buf, adj, sems):
    step = pl.program_id(0)
    tiles = dest_ref.shape[0]
    per_unit = nb * nb
    chunks = sems.shape[0]
    size = tiles // chunks
    me = lax.axis_index("row")

    def fetch(c):
        part = pl.ds(c * size, size)
        return pltpu.make_async_copy(pat_hbm.at[part], buf.at[part], sems.at[c])

    @pl.when(step == 0)
    def _():
        for c in range(chunks):
            fetch(c).start()

    def clear(i, carry):
        adj[pl.ds(i * per_unit, per_unit)] = jnp.zeros((per_unit,) + adj.shape[1:], BF16)
        return carry

    lax.fori_loop(0, group, clear, 0)
    for c in range(chunks):

        @pl.when(step == 0)
        def _(c=c):
            fetch(c).wait()

        def add(i, carry, c=c):
            t = c * size + i
            unit = dest_ref[t] ^ me
            place = ((unit - step * group) * nb + dst_ref[t]) * nb + src_ref[t]

            def store():
                adj[place] += buf[t].astype(F32).astype(BF16)

            if split:
                pl.when((place >= 0) & (place < group * per_unit))(store)
            else:
                store()
            return carry

        lax.fori_loop(0, size, add, 0)


def forward_kernel(
    nb, group, split, parts, dest_ref, src_ref, dst_ref, x_hbm, pat_hbm, *refs
):
    outs, (x_vmem, buf, adj, odd, even, sems, x_sem, out_sems) = refs[:-8], refs[-8:]
    tile = adj.shape[1]
    rows = x_vmem.shape[0]
    copy = pltpu.make_async_copy(x_hbm, x_vmem, x_sem)
    copy.start()
    build(nb, group, split, dest_ref, src_ref, dst_ref, pat_hbm, buf, adj, sems)
    copy.wait()
    xt = x_vmem[...].T
    width = 2 if nb % 2 == 0 else 1
    half = group // 2
    step = pl.program_id(0)
    copies = []
    for units, out_hbm in zip((*parts, range(half)), outs, strict=True):
        parity = 0 if out_hbm is outs[-1] else 1
        sums = odd if parity else even
        for place, m in enumerate(units):
            for k in range(0, nb, width):
                weight = jnp.concatenate(
                    [
                        adj[pl.ds(((2 * m + parity) * nb + k + j) * nb, nb)].reshape(rows, tile)
                        for j in range(width)
                    ],
                    axis=1,
                )
                sums[m, :, k * tile : (k + width) * tile] = jnp.dot(
                    xt, weight, preferred_element_type=F32
                ).astype(sums.dtype)
            copy = pltpu.make_async_copy(
                sums.at[m], out_hbm.at[step * half + place], out_sems.at[parity, m]
            )
            copy.start()
            copies.append(copy)
    for copy in copies:
        copy.wait()


def forward_sums(units, own_dtype, tiles_at, features, patterns, nb, parts):
    rows, feat = features.shape
    tiles, tile, _ = patterns.shape
    group = min(2 * GROUP, units)
    any_space = pl.BlockSpec(memory_space=pl.ANY)
    steps = units // group
    return pl.pallas_call(
        functools.partial(forward_kernel, nb, group, units > group, parts),
        grid=(steps,),
        in_specs=[pl.BlockSpec(memory_space=pltpu.SMEM)] * 3 + [any_space, any_space],
        out_specs=[any_space] * (len(parts) + 1),
        scratch_shapes=[
            pltpu.VMEM((rows, feat), BF16),
            pltpu.VMEM((tiles, tile, tile), jnp.int32),
            pltpu.VMEM((group * nb * nb, tile, tile), BF16),
            pltpu.VMEM((group // 2, feat, rows), BF16),
            pltpu.VMEM((group // 2, feat, rows), own_dtype),
            pltpu.SemaphoreType.DMA((CHUNKS,)),
            pltpu.SemaphoreType.DMA,
            pltpu.SemaphoreType.DMA((2, group // 2)),
        ],
        out_shape=[jax.ShapeDtypeStruct((len(p) * steps, feat, rows), BF16) for p in parts]
        + [jax.ShapeDtypeStruct((units // 2, feat, rows), own_dtype)],
        compiler_params=pltpu.CompilerParams(vmem_limit_bytes=PLAN["k1l"] * MIB),
        cost_estimate=LIGHT,
        name="forward_sums",
    )(*tiles_at, features, patterns)


def adjacency_kernel(
    nb, group, split, dest_ref, src_ref, dst_ref, pat_hbm, after_hbm, adj, made_ref, *scratch
):
    buf, sems = scratch
    made_ref[...] = jnp.zeros(made_ref.shape, F32)
    build(nb, group, split, dest_ref, src_ref, dst_ref, pat_hbm, buf, adj, sems)


def adjacency(units, tiles_at, patterns, nb, after):
    tiles, tile, _ = patterns.shape
    group = min(2 * GROUP, units)
    any_space = pl.BlockSpec(memory_space=pl.ANY)
    blocks = group * nb * nb
    if units > group:
        out_spec = pl.BlockSpec((blocks, tile, tile), lambda g: (g, 0, 0))
    else:
        out_spec = pl.BlockSpec(memory_space=pltpu.VMEM)
    return pl.pallas_call(
        functools.partial(adjacency_kernel, nb, group, units > group),
        grid=(units // group,),
        in_specs=[pl.BlockSpec(memory_space=pltpu.SMEM)] * 3 + [any_space, any_space],
        out_specs=[out_spec, pl.BlockSpec((8, 128), lambda g: (0, 0))],
        scratch_shapes=[
            pltpu.VMEM((tiles, tile, tile), jnp.int32),
            pltpu.SemaphoreType.DMA((CHUNKS,)),
        ],
        out_shape=[
            jax.ShapeDtypeStruct((units * nb * nb, tile, tile), BF16),
            jax.ShapeDtypeStruct((8, 128), F32),
        ],
        compiler_params=pltpu.CompilerParams(vmem_limit_bytes=PLAN["adjl"] * MIB),
        cost_estimate=HEAVY if PLAN["adj"] else LIGHT,
        name="adjacency",
    )(*tiles_at, patterns, after)


def add_kernel(n, total_ref, *refs):
    total = total_ref[0].astype(F32)
    for r in refs[:n]:
        total += r[0].astype(F32)
    refs[-1][0] = total


def add_first(total, parts, after):
    block = (1,) + total.shape[1:]
    spec = pl.BlockSpec(block, lambda i: (0, 0, 0))
    return pl.pallas_call(
        functools.partial(add_kernel, len(parts)),
        grid=(1,),
        in_specs=[spec] * (1 + len(parts)) + [pl.BlockSpec(memory_space=pl.ANY)],
        out_specs=spec,
        out_shape=jax.ShapeDtypeStruct(block, F32),
        compiler_params=pltpu.CompilerParams(vmem_limit_bytes=8 * MIB),
        cost_estimate=HEAVY if PLAN["ph"] else LIGHT,
        name="add_first",
    )(total, *parts, after)


def layer_kernel(n_recv, made_hbm, own_ref, *refs):
    recv = refs[:n_recv]
    (deg_ref, x_ref, cot_ref, ws_ref, wn_ref, bias_ref) = refs[n_recv : n_recv + 6]
    out_ref, delta_ref, aggt_ref, back_ref = refs[n_recv + 6 :]
    total = own_ref[0].astype(F32)
    for r in recv:
        total += r[...].reshape(total.shape).astype(F32)
    degree = 1.0 + deg_ref[...].astype(F32)
    degree = jnp.broadcast_to(degree, total.shape)
    aggt = (total / degree).astype(BF16)
    aggt_ref[...] = aggt
    agg = aggt.T
    pre = (
        jnp.dot(x_ref[...], ws_ref[...], preferred_element_type=F32)
        + jnp.dot(agg, wn_ref[...], preferred_element_type=F32)
        + bias_ref[...]
    )
    sigma = jax.nn.sigmoid(pre)
    out_ref[...] = (pre * sigma).astype(BF16)
    delta = (cot_ref[...].astype(F32) * sigma * (1.0 + pre * (1.0 - sigma))).astype(BF16)
    delta_ref[...] = delta
    back = lax.dot_general(
        delta, wn_ref[...], (((1,), (1,)), ((), ())), preferred_element_type=F32
    )
    back_ref[...] = (back / degree.T).astype(BF16)


def layer(made, own, recv, in_degree, features, cotangent, w_self, w_neigh, bias):
    rows, feat = features.shape
    hidden = w_self.shape[1]

    def first(a):
        return pl.BlockSpec((1,) + a.shape[1:], lambda i: (0, 0, 0))

    def whole(a):
        return pl.BlockSpec(a.shape, lambda i, n=a.ndim: (0,) * n)

    rest = [in_degree, features, cotangent, w_self, w_neigh, bias]
    return pl.pallas_call(
        functools.partial(layer_kernel, len(recv)),
        grid=(1,),
        in_specs=[pl.BlockSpec(memory_space=pl.ANY), first(own)]
        + [first(r) for r in recv]
        + [whole(a) for a in rest],
        out_specs=[
            pl.BlockSpec((rows, hidden), lambda i: (0, 0)),
            pl.BlockSpec((rows, hidden), lambda i: (0, 0)),
            pl.BlockSpec((feat, rows), lambda i: (0, 0)),
            pl.BlockSpec((rows, feat), lambda i: (0, 0)),
        ],
        out_shape=[
            jax.ShapeDtypeStruct((rows, hidden), BF16),
            jax.ShapeDtypeStruct((rows, hidden), BF16),
            jax.ShapeDtypeStruct((feat, rows), BF16),
            jax.ShapeDtypeStruct((rows, feat), BF16),
        ],
        compiler_params=pltpu.CompilerParams(vmem_limit_bytes=8 * MIB),
        cost_estimate=LIGHT,
        name="layer",
    )(made, own, *recv, *rest)


def grad_kernel(scale, me_ref, x_ref, delta_ref, aggt_ref, ws_ref, g_ref, base_ref):
    delta = delta_ref[...]
    feat = x_ref.shape[1]
    gs = jnp.dot(x_ref[...].T, delta, preferred_element_type=F32) * scale
    gn = jnp.dot(aggt_ref[...], delta, preferred_element_type=F32) * scale
    gb = jnp.sum(delta.astype(F32), axis=0, keepdims=True) * scale
    gb = jnp.broadcast_to(gb, (8, gb.shape[1]))
    core = me_ref[0] % 2
    half = feat // 2
    for h in range(2):
        place = core ^ h
        g_ref[place, 0:half] = gs[h * half : (h + 1) * half]
        g_ref[place, half:feat] = gn[h * half : (h + 1) * half]
        g_ref[place, feat : feat + 8] = gb
    base_ref[...] = lax.dot_general(
        delta, ws_ref[...], (((1,), (1,)), ((), ())), preferred_element_type=F32
    )


def grad_terms(scale, me, features, delta, aggt, w_self):
    rows, feat = features.shape
    hidden = delta.shape[1]
    vm = pl.BlockSpec(memory_space=pltpu.VMEM)
    return pl.pallas_call(
        functools.partial(grad_kernel, scale),
        in_specs=[pl.BlockSpec(memory_space=pltpu.SMEM), vm, vm, vm, vm],
        out_specs=[vm, vm],
        out_shape=[
            jax.ShapeDtypeStruct((2, feat + 8, hidden), F32),
            jax.ShapeDtypeStruct((rows, feat), F32),
        ],
        compiler_params=pltpu.CompilerParams(vmem_limit_bytes=8 * MIB),
        cost_estimate=LIGHT,
        name="grad_terms",
    )(me, features, delta, aggt, w_self)


def spread_kernel(places, nb, n_arrays, marks, acc_ref, adj_hbm, *refs):
    refs = refs[marks:]
    backs = refs[:n_arrays]
    out_ref, adj, sems = refs[n_arrays], *refs[-2:]
    per_unit = nb * nb
    copies = []
    for i, place in enumerate(places):
        copy = pltpu.make_async_copy(
            adj_hbm.at[pl.ds(place * per_unit, per_unit)], adj.at[i], sems.at[i]
        )
        copy.start()
        copies.append(copy)
    total = acc_ref[...]
    rows = total.shape[0]
    i = 0
    for back in backs:
        for j in range(back.shape[0]):
            copies[i].wait()
            tile = adj.shape[2]
            left = jnp.concatenate(
                [adj[i, k * nb : (k + 1) * nb].reshape(rows, tile) for k in range(nb)], axis=1
            )
            total += jnp.dot(left, back[j], preferred_element_type=F32)
            i += 1
    out_ref[...] = total.astype(out_ref.dtype)


def gate_kernel(*refs):
    refs[-1][...] = jnp.zeros(refs[-1].shape, F32)


def gate(*arrays):
    return pl.pallas_call(
        gate_kernel,
        in_specs=[pl.BlockSpec(memory_space=pl.ANY)] * len(arrays),
        out_specs=pl.BlockSpec(memory_space=pltpu.VMEM),
        out_shape=jax.ShapeDtypeStruct((8, 128), F32),
        compiler_params=pltpu.CompilerParams(vmem_limit_bytes=4 * MIB),
        cost_estimate=HEAVY,
        name="gate",
    )(*arrays)


def finish_kernel(me_ref, mine_ref, theirs_ref, *refs):
    gs_ref, gn_ref, gb_ref = refs[-3:]
    feat = gs_ref.shape[0]
    half = feat // 2
    core = me_ref[0] % 2
    for other, ref in ((0, mine_ref), (1, theirs_ref)):
        at = pl.ds(pl.multiple_of((core ^ other) * half, half), half)
        gs_ref[at] = ref[0:half]
        gn_ref[at] = ref[half:feat]
    gb_ref[...] = mine_ref[feat : feat + 1]


def finish(me, mine, theirs, after):
    vm = pl.BlockSpec(memory_space=pltpu.VMEM)
    rows, hidden = mine.shape
    feat = rows - 8
    return pl.pallas_call(
        finish_kernel,
        in_specs=[pl.BlockSpec(memory_space=pltpu.SMEM), vm, vm]
        + [pl.BlockSpec(memory_space=pl.ANY)] * len(after),
        out_specs=[vm] * 3,
        out_shape=[
            jax.ShapeDtypeStruct((feat, hidden), F32),
            jax.ShapeDtypeStruct((feat, hidden), F32),
            jax.ShapeDtypeStruct((1, hidden), F32),
        ],
        compiler_params=pltpu.CompilerParams(vmem_limit_bytes=4 * MIB),
        cost_estimate=LIGHT,
        name="finish",
    )(me, mine, theirs, *after)


def last_kernel(
    places, nb, n_arrays, marks, me_ref, mine_ref, theirs_ref, acc_ref, adj_hbm, *refs
):
    refs = refs[marks:]
    backs, out_ref, grads, scratch = refs[:n_arrays], refs[n_arrays], refs[-5:-2], refs[-2:]
    finish_kernel(me_ref, mine_ref, theirs_ref, *grads)
    spread_kernel(places, nb, n_arrays, 0, acc_ref, adj_hbm, *backs, out_ref, *scratch)


def spread(acc, adjacency, marks, places, backs, nb, dtype, heavy=True, grads=None):
    vm = pl.BlockSpec(memory_space=pltpu.VMEM)
    rows, feat = acc.shape
    per_unit = nb * nb
    tile = adjacency.shape[1]
    n = len(places)
    any_space = pl.BlockSpec(memory_space=pl.ANY)
    in_specs = [vm, any_space] + [any_space] * len(marks) + [vm] * len(backs)
    inputs = [acc, adjacency, *marks, *backs]
    kernel, out_shape = spread_kernel, jax.ShapeDtypeStruct((rows, feat), dtype)
    if grads is not None:
        in_specs = [pl.BlockSpec(memory_space=pltpu.SMEM), vm, vm] + in_specs
        inputs = [*grads, *inputs]
        hidden = grads[1].shape[1]
        kernel = last_kernel
        out_shape = [
            out_shape,
            jax.ShapeDtypeStruct((feat, hidden), F32),
            jax.ShapeDtypeStruct((feat, hidden), F32),
            jax.ShapeDtypeStruct((1, hidden), F32),
        ]
    return pl.pallas_call(
        functools.partial(kernel, tuple(places), nb, len(backs), len(marks)),
        in_specs=in_specs,
        out_specs=jax.tree.map(lambda _: vm, out_shape),
        out_shape=out_shape,
        scratch_shapes=[
            pltpu.VMEM((n, per_unit, tile, tile), BF16),
            pltpu.SemaphoreType.DMA((n,)),
        ],
        compiler_params=pltpu.CompilerParams(vmem_limit_bytes=12 * MIB),
        cost_estimate=HEAVY if heavy else LIGHT,
        name="spread",
    )(*inputs)


def tree_sum(values):
    while len(values) > 1:
        values = [values[i] + values[i + 1] for i in range(0, len(values), 2)]
    return values[0]


def stages_of(devices):
    bits = devices.bit_length() - 1
    assert 1 << bits == devices and bits >= 3
    rest = bits - 1
    return rest // 2, rest - rest // 2


def on_device(
    features,
    patterns,
    tile_dest,
    tile_src_block,
    tile_dst_block,
    in_degree,
    w_self,
    w_neigh,
    bias,
    cotangent,
):
    devices = lax.axis_size("row")
    me = lax.axis_index("row")
    tile = patterns.shape[1]
    rows, feat = features.shape
    nb = rows // tile
    y_bits, z_bits = stages_of(devices)
    ny, nz = 1 << y_bits, 1 << z_bits
    units = devices // 2
    small = devices == 16

    tiles_at = (tile_dest.reshape(-1), tile_src_block, tile_dst_block)

    parts = PLAN["halves"] if small else (tuple(range(min(GROUP, units))),)
    *s_other, s_own = forward_sums(
        devices, F32 if small else BF16, tiles_at, features, patterns, nb, parts
    )
    received = [swap(s, 1, devices) for s in s_other]
    s_recv = received[-1]
    from_other = {}
    for units_of, got in zip(parts, received, strict=True):
        if small:
            from_other.update({m: got[i] for i, m in enumerate(units_of)})
    if not small:
        from_other = {m: s_recv[m] for m in range(units)}

    def chip_sum(m):
        return s_own[m].astype(F32) + from_other[m].astype(F32)

    if small:
        y_recv = [None] * nz
        sent = None
        for n in PLAN["y"]:
            y_recv[n] = []
            if n in PLAN["direct"]:
                continue
            for k in range(1, ny):
                own, recv = s_own[n * ny + k], from_other[n * ny + k]
                if sent is not None and PLAN["ysep"]:
                    own, recv, sent = lax.optimization_barrier((own, recv, sent))
                sent = (own.astype(F32) + recv.astype(F32)).astype(BF16)
                y_recv[n].append(swap(sent, 2 * k, devices))
    else:
        s5 = s_own.reshape(nz, ny, feat, rows)
        r5 = s_recv.reshape(nz, ny, feat, rows)
        got = [
            swap((s5[:, k].astype(F32) + r5[:, k].astype(F32)).astype(BF16), 2 * k, devices)
            for k in range(1, ny)
        ]
        y_recv = [[g[n] for g in got] for n in range(nz)]
    z_recv = {}
    sent = None
    sums, first_sent, sent = {}, sent if small else None, None
    for n in PLAN["z"] if small else reversed(range(1, nz)):
        arrived = y_recv[n]
        if small and n in PLAN["direct"]:
            for k in range(ny):
                m = n * ny + k
                mine, recv, sent = s_own[m], from_other[m], first_sent
                if PLAN["dsep"]:
                    mine, recv, sent = lax.optimization_barrier((mine, recv, sent))
                direct = (mine.astype(F32) + recv.astype(F32)).astype(BF16)
                z_recv[m / ny] = swap(direct, 2 * m, devices)[None]
            continue
        if sent is not None:
            arrived, sent = lax.optimization_barrier((arrived, sent))
        total = chip_sum(n * ny)
        for r in arrived:
            total = total + r.astype(F32)
        sums[n] = sent = total.astype(BF16)
        z_recv[n] = swap(sent, 2 * ny * n, devices)[None]
    after = PLAN["after"] if small else 1
    made = s_recv
    if after == 4:
        adj, made = adjacency(devices, tiles_at, patterns, nb, z_recv[3])
    elif after:
        adj, made = adjacency(devices, tiles_at, patterns, nb, sums[after])
    total, summed = s_own, ()
    parts = PLAN["parts"] if small else [(n,) for n in range(2, nz)]
    for i, part in enumerate(parts):
        extra = [s_recv] if i == 0 else []
        total = add_first(total, extra + [z_recv[n] for n in part], made)
        summed += part
    if not parts:
        summed = ()
    rest = [z_recv[n] for n in z_recv if n not in summed]

    output, delta, aggt, back = layer(
        made,
        total,
        ([s_recv] if not parts else []) + [r[None] for r in y_recv[0]] + rest,
        in_degree.reshape(1, rows),
        features,
        cotangent,
        w_self,
        w_neigh,
        bias.reshape(1, -1),
    )
    if not after:
        adj, made = adjacency(devices, tiles_at, patterns, nb, back)
    me = me.reshape(1).astype(jnp.int32)
    scale = 1.0 / math.sqrt(rows * devices)
    terms, base = grad_terms(scale, me, features, delta, aggt, w_self)

    have = {0: back}
    for n in PLAN["agz"] if small else range(1, nz):
        have[n * ny] = swap(back, 2 * ny * n, devices)
    own = {0: back[None]}
    onward = []
    for n in range(nz):
        own[2 * n * ny] = have[n * ny][None]
        for k in range(1, ny):
            m = n * ny + k
            if small and n in PLAN["agd"]:
                own[2 * m] = swap(back, 2 * m, devices)[None]
            elif small and PLAN["yfs"] and n > 0:
                onward.append(n)
            else:
                own[2 * m] = swap(have[n * ny], 2 * k, devices)[None]
    if onward:
        key = tuple(2 * n * ny + 2 for n in onward)
        own[key] = swap(jnp.stack([have[n * ny] for n in onward]), 2, devices)

    def plus_one(key):
        return tuple(u + 1 for u in key) if isinstance(key, tuple) else (key + 1,)

    across = {}
    for keys in PLAN["pairs"] if small else [(key,) for key in own]:
        name = sum((plus_one(key) for key in keys), ())
        parts = [own[key] for key in keys]
        whole = jnp.concatenate(parts, axis=0) if len(parts) > 1 else parts[0]
        across[name] = swap(whole, 1, devices)

    def later(value, what):
        key = PLAN[what]
        if key is None or not small:
            return value
        value, own[key] = lax.optimization_barrier((value, own[key]))
        return value

    terms = later(terms, "terms")
    half = terms[0] + swap(terms[1], 1, devices)
    half = later(half, "gy")
    if PLAN["gyb"]:
        half = half.astype(BF16)
    half = tree_sum(
        [half.astype(F32)] + [swap(half, 2 * k, devices).astype(F32) for k in range(1, ny)]
    )
    half = later(half, "gz")
    y_half = half
    if PLAN["butter"] and small:
        for n in (1, 2):
            rounded = half.astype(BF16)
            half = rounded.astype(F32) + swap(rounded, 2 * ny * n, devices).astype(F32)
    else:
        rounded = half.astype(BF16)
        half = tree_sum(
            [rounded.astype(F32)]
            + [swap(rounded, 2 * ny * n, devices).astype(F32) for n in range(1, nz)]
        )
    second = swap(half, 1, devices)

    if small:
        groups, heavy = PLAN["groups"], PLAN["heavy"]
    else:
        singles = list(own) + list(across)
        groups = [singles[at : at + GROUP] for at in range(0, devices, GROUP)]
        heavy = [1] * len(groups)
    grad_feat = base
    for i, group in enumerate(groups):
        last = i == len(groups) - 1
        parts = [(u, own[u]) if u in own else (u, across[u]) for u in group]
        parts = [(u if isinstance(u, tuple) else (u,), b) for u, b in parts]
        places = [u for us, _ in parts for u in us]
        marks = []
        for at, keys, with_half in PLAN["gates"] if small else ():
            if at == i:
                marks.append(gate(*([grad_feat] if i else []), *[own[k] if k in own else across[k] for k in keys], *([y_half] if with_half else [])))
        grad_feat = spread(
            grad_feat,
            adj,
            marks,
            places,
            [b for _, b in parts],
            nb,
            BF16 if last else F32,
            heavy[i],
            (me, half, second) if last and PLAN["fin"] else None,
        )
    if PLAN["fin"]:
        grad_feat, grad_self, grad_neigh, grad_bias = grad_feat
    else:
        grad_self, grad_neigh, grad_bias = finish(me, half, second, [grad_feat] if PLAN["findep"] else [])
    return (output, grad_feat, grad_self, grad_neigh, grad_bias.reshape(-1))


def solution(mesh):
    return jax.shard_map(
        on_device,
        mesh=mesh,
        in_specs=(
            P(("grp", "row"), None),
            P(("grp", "row"), None, None),
            P(("grp", "row"), None),
            P(("grp", "row")),
            P(("grp", "row")),
            P(("grp", "row")),
            P(),
            P(),
            P(),
            P(("grp", "row"), None),
        ),
        out_specs=(
            P(("grp", "row"), None),
            P(("grp", "row"), None),
            P("grp", None),
            P("grp", None),
            P("grp"),
        ),
        check_vma=False,
    )
```

```python
import functools
import math

import jax
import jax.numpy as jnp
from jax import lax
from jax.experimental import pallas as pl
from jax.experimental.pallas import tpu as pltpu
from jax.sharding import PartitionSpec as P

BF16 = jnp.bfloat16
F32 = jnp.float32
GROUP = 8
CHUNKS = 16
MIB = 1 << 20
PLAN = {'z': (1, 3, 2), 'y': (3, 2, 1, 0), 'parts': (), 'token': 0, 'after': 4, 'adj': 1, 'ysep': 1, 'agz': (3, 2, 1), 'groups': ((0,), (12, 4, 2, 8, 6, (1,), (3,), (5,)), (14, 10, (13,), (9,), (7,)), ((15,), (11,))), 'heavy': (1, 1, 1, 1), 'pairs': ((0,), (2,), (4,), (6,), (8,), (12,), (10,), (14,)), 'terms': None, 'gy': None, 'gz': None, 'butter': 0, 'fin': 1, 'ph': 0, 'findep': 0, 'gyb': 1, 'direct': (1,), 'yfs': 0, 'agd': (1,), 'dsep': 0, 'k1l': 55, 'adjl': 38, 'gates': ((1, (12, 4, 2, 8), 1),), 'halves': ((7, 5, 2, 3), (0, 6, 4, 1))}
LIGHT = pl.CostEstimate(flops=0, bytes_accessed=0, transcendentals=0)
HEAVY = pl.CostEstimate(flops=20_000_000_000, bytes_accessed=0, transcendentals=0)


def swap(value, bits, devices):
    return lax.ppermute(value, "row", [(i, i ^ bits) for i in range(devices)])


def build(nb, group, split, dest_ref, src_ref, dst_ref, pat_hbm, buf, adj, sems):
    step = pl.program_id(0)
    tiles = dest_ref.shape[0]
    per_unit = nb * nb
    chunks = sems.shape[0]
    size = tiles // chunks
    me = lax.axis_index("row")

    def fetch(c):
        part = pl.ds(c * size, size)
        return pltpu.make_async_copy(pat_hbm.at[part], buf.at[part], sems.at[c])

    @pl.when(step == 0)
    def _():
        for c in range(chunks):
            fetch(c).start()

    def clear(i, carry):
        adj[pl.ds(i * per_unit, per_unit)] = jnp.zeros((per_unit,) + adj.shape[1:], BF16)
        return carry

    lax.fori_loop(0, group, clear, 0, unroll=2)
    for c in range(chunks):

        @pl.when(step == 0)
        def _(c=c):
            fetch(c).wait()

        def add(i, carry, c=c):
            t = c * size + i
            unit = dest_ref[t] ^ me
            place = ((unit - step * group) * nb + dst_ref[t]) * nb + src_ref[t]

            def store():
                adj[place] += buf[t].astype(F32).astype(BF16)

            if split:
                pl.when((place >= 0) & (place < group * per_unit))(store)
            else:
                store()
            return carry

        lax.fori_loop(0, size, add, 0, unroll=2)


def forward_kernel(
    nb, group, split, parts, dest_ref, src_ref, dst_ref, x_hbm, pat_hbm, *refs
):
    outs, (x_vmem, buf, adj, odd, even, sems, x_sem, out_sems) = refs[:-8], refs[-8:]
    tile = adj.shape[1]
    rows = x_vmem.shape[0]
    copy = pltpu.make_async_copy(x_hbm, x_vmem, x_sem)
    copy.start()
    build(nb, group, split, dest_ref, src_ref, dst_ref, pat_hbm, buf, adj, sems)
    copy.wait()
    xt = x_vmem[...].T
    width = 2 if nb % 2 == 0 else 1
    half = group // 2
    step = pl.program_id(0)
    copies = []
    for units, out_hbm in zip((*parts, range(half)), outs, strict=True):
        parity = 0 if out_hbm is outs[-1] else 1
        sums = odd if parity else even
        for place, m in enumerate(units):
            for k in range(0, nb, width):
                weight = jnp.concatenate(
                    [
                        adj[pl.ds(((2 * m + parity) * nb + k + j) * nb, nb)].reshape(rows, tile)
                        for j in range(width)
                    ],
                    axis=1,
                )
                sums[m, :, k * tile : (k + width) * tile] = jnp.dot(
                    xt, weight, preferred_element_type=F32
                ).astype(sums.dtype)
            copy = pltpu.make_async_copy(
                sums.at[m], out_hbm.at[step * half + place], out_sems.at[parity, m]
            )
            copy.start()
            copies.append(copy)
    for copy in copies:
        copy.wait()


def forward_sums(units, own_dtype, tiles_at, features, patterns, nb, parts):
    rows, feat = features.shape
    tiles, tile, _ = patterns.shape
    group = min(2 * GROUP, units)
    any_space = pl.BlockSpec(memory_space=pl.ANY)
    steps = units // group
    return pl.pallas_call(
        functools.partial(forward_kernel, nb, group, units > group, parts),
        grid=(steps,),
        in_specs=[pl.BlockSpec(memory_space=pltpu.SMEM)] * 3 + [any_space, any_space],
        out_specs=[any_space] * (len(parts) + 1),
        scratch_shapes=[
            pltpu.VMEM((rows, feat), BF16),
            pltpu.VMEM((tiles, tile, tile), jnp.int32),
            pltpu.VMEM((group * nb * nb, tile, tile), BF16),
            pltpu.VMEM((group // 2, feat, rows), BF16),
            pltpu.VMEM((group // 2, feat, rows), own_dtype),
            pltpu.SemaphoreType.DMA((CHUNKS,)),
            pltpu.SemaphoreType.DMA,
            pltpu.SemaphoreType.DMA((2, group // 2)),
        ],
        out_shape=[jax.ShapeDtypeStruct((len(p) * steps, feat, rows), BF16) for p in parts]
        + [jax.ShapeDtypeStruct((units // 2, feat, rows), own_dtype)],
        compiler_params=pltpu.CompilerParams(vmem_limit_bytes=PLAN["k1l"] * MIB),
        cost_estimate=LIGHT,
        name="forward_sums",
    )(*tiles_at, features, patterns)


def adjacency_kernel(
    nb, group, split, dest_ref, src_ref, dst_ref, pat_hbm, after_hbm, adj, made_ref, *scratch
):
    buf, sems = scratch
    made_ref[...] = jnp.zeros(made_ref.shape, F32)
    build(nb, group, split, dest_ref, src_ref, dst_ref, pat_hbm, buf, adj, sems)


def adjacency(units, tiles_at, patterns, nb, after):
    tiles, tile, _ = patterns.shape
    group = min(2 * GROUP, units)
    any_space = pl.BlockSpec(memory_space=pl.ANY)
    blocks = group * nb * nb
    if units > group:
        out_spec = pl.BlockSpec((blocks, tile, tile), lambda g: (g, 0, 0))
    else:
        out_spec = pl.BlockSpec(memory_space=pltpu.VMEM)
    return pl.pallas_call(
        functools.partial(adjacency_kernel, nb, group, units > group),
        grid=(units // group,),
        in_specs=[pl.BlockSpec(memory_space=pltpu.SMEM)] * 3 + [any_space, any_space],
        out_specs=[out_spec, pl.BlockSpec((8, 128), lambda g: (0, 0))],
        scratch_shapes=[
            pltpu.VMEM((tiles, tile, tile), jnp.int32),
            pltpu.SemaphoreType.DMA((CHUNKS,)),
        ],
        out_shape=[
            jax.ShapeDtypeStruct((units * nb * nb, tile, tile), BF16),
            jax.ShapeDtypeStruct((8, 128), F32),
        ],
        compiler_params=pltpu.CompilerParams(vmem_limit_bytes=PLAN["adjl"] * MIB),
        cost_estimate=HEAVY if PLAN["adj"] else LIGHT,
        name="adjacency",
    )(*tiles_at, patterns, after)


def add_kernel(n, total_ref, *refs):
    total = total_ref[0].astype(F32)
    for r in refs[:n]:
        total += r[0].astype(F32)
    refs[-1][0] = total


def add_first(total, parts, after):
    block = (1,) + total.shape[1:]
    spec = pl.BlockSpec(block, lambda i: (0, 0, 0))
    return pl.pallas_call(
        functools.partial(add_kernel, len(parts)),
        grid=(1,),
        in_specs=[spec] * (1 + len(parts)) + [pl.BlockSpec(memory_space=pl.ANY)],
        out_specs=spec,
        out_shape=jax.ShapeDtypeStruct(block, F32),
        compiler_params=pltpu.CompilerParams(vmem_limit_bytes=8 * MIB),
        cost_estimate=HEAVY if PLAN["ph"] else LIGHT,
        name="add_first",
    )(total, *parts, after)


def layer_kernel(n_recv, made_hbm, own_ref, *refs):
    recv = refs[:n_recv]
    (deg_ref, x_ref, cot_ref, ws_ref, wn_ref, bias_ref) = refs[n_recv : n_recv + 6]
    out_ref, delta_ref, aggt_ref, back_ref = refs[n_recv + 6 :]
    total = own_ref[0].astype(F32)
    for r in recv:
        total += r[...].reshape(total.shape).astype(F32)
    degree = 1.0 + deg_ref[...].astype(F32)
    degree = jnp.broadcast_to(degree, total.shape)
    aggt = (total / degree).astype(BF16)
    aggt_ref[...] = aggt
    agg = aggt.T
    pre = (
        jnp.dot(x_ref[...], ws_ref[...], preferred_element_type=F32)
        + jnp.dot(agg, wn_ref[...], preferred_element_type=F32)
        + bias_ref[...]
    )
    sigma = jax.nn.sigmoid(pre)
    out_ref[...] = (pre * sigma).astype(BF16)
    delta = (cot_ref[...].astype(F32) * sigma * (1.0 + pre * (1.0 - sigma))).astype(BF16)
    delta_ref[...] = delta
    back = lax.dot_general(
        delta, wn_ref[...], (((1,), (1,)), ((), ())), preferred_element_type=F32
    )
    back_ref[...] = (back / degree.T).astype(BF16)


def layer(made, own, recv, in_degree, features, cotangent, w_self, w_neigh, bias):
    rows, feat = features.shape
    hidden = w_self.shape[1]

    def first(a):
        return pl.BlockSpec((1,) + a.shape[1:], lambda i: (0, 0, 0))

    def whole(a):
        return pl.BlockSpec(a.shape, lambda i, n=a.ndim: (0,) * n)

    rest = [in_degree, features, cotangent, w_self, w_neigh, bias]
    return pl.pallas_call(
        functools.partial(layer_kernel, len(recv)),
        grid=(1,),
        in_specs=[pl.BlockSpec(memory_space=pl.ANY), first(own)]
        + [first(r) for r in recv]
        + [whole(a) for a in rest],
        out_specs=[
            pl.BlockSpec((rows, hidden), lambda i: (0, 0)),
            pl.BlockSpec((rows, hidden), lambda i: (0, 0)),
            pl.BlockSpec((feat, rows), lambda i: (0, 0)),
            pl.BlockSpec((rows, feat), lambda i: (0, 0)),
        ],
        out_shape=[
            jax.ShapeDtypeStruct((rows, hidden), BF16),
            jax.ShapeDtypeStruct((rows, hidden), BF16),
            jax.ShapeDtypeStruct((feat, rows), BF16),
            jax.ShapeDtypeStruct((rows, feat), BF16),
        ],
        compiler_params=pltpu.CompilerParams(vmem_limit_bytes=8 * MIB),
        cost_estimate=LIGHT,
        name="layer",
    )(made, own, *recv, *rest)


def grad_kernel(scale, me_ref, x_ref, delta_ref, aggt_ref, ws_ref, g_ref, base_ref):
    delta = delta_ref[...]
    feat = x_ref.shape[1]
    gs = jnp.dot(x_ref[...].T, delta, preferred_element_type=F32) * scale
    gn = jnp.dot(aggt_ref[...], delta, preferred_element_type=F32) * scale
    gb = jnp.sum(delta.astype(F32), axis=0, keepdims=True) * scale
    gb = jnp.broadcast_to(gb, (8, gb.shape[1]))
    core = me_ref[0] % 2
    half = feat // 2
    for h in range(2):
        place = core ^ h
        g_ref[place, 0:half] = gs[h * half : (h + 1) * half]
        g_ref[place, half:feat] = gn[h * half : (h + 1) * half]
        g_ref[place, feat : feat + 8] = gb
    base_ref[...] = lax.dot_general(
        delta, ws_ref[...], (((1,), (1,)), ((), ())), preferred_element_type=F32
    )


def grad_terms(scale, me, features, delta, aggt, w_self):
    rows, feat = features.shape
    hidden = delta.shape[1]
    vm = pl.BlockSpec(memory_space=pltpu.VMEM)
    return pl.pallas_call(
        functools.partial(grad_kernel, scale),
        in_specs=[pl.BlockSpec(memory_space=pltpu.SMEM), vm, vm, vm, vm],
        out_specs=[vm, vm],
        out_shape=[
            jax.ShapeDtypeStruct((2, feat + 8, hidden), F32),
            jax.ShapeDtypeStruct((rows, feat), F32),
        ],
        compiler_params=pltpu.CompilerParams(vmem_limit_bytes=8 * MIB),
        cost_estimate=LIGHT,
        name="grad_terms",
    )(me, features, delta, aggt, w_self)


def spread_kernel(places, nb, n_arrays, marks, acc_ref, adj_hbm, *refs):
    refs = refs[marks:]
    backs = refs[:n_arrays]
    out_ref, adj, sems = refs[n_arrays], *refs[-2:]
    per_unit = nb * nb
    copies = []
    for i, place in enumerate(places):
        copy = pltpu.make_async_copy(
            adj_hbm.at[pl.ds(place * per_unit, per_unit)], adj.at[i], sems.at[i]
        )
        copy.start()
        copies.append(copy)
    total = acc_ref[...]
    rows = total.shape[0]
    i = 0
    for back in backs:
        for j in range(back.shape[0]):
            copies[i].wait()
            tile = adj.shape[2]
            left = jnp.concatenate(
                [adj[i, k * nb : (k + 1) * nb].reshape(rows, tile) for k in range(nb)], axis=1
            )
            total += jnp.dot(left, back[j], preferred_element_type=F32)
            i += 1
    out_ref[...] = total.astype(out_ref.dtype)


def gate_kernel(*refs):
    refs[-1][...] = jnp.zeros(refs[-1].shape, F32)


def gate(*arrays):
    return pl.pallas_call(
        gate_kernel,
        in_specs=[pl.BlockSpec(memory_space=pl.ANY)] * len(arrays),
        out_specs=pl.BlockSpec(memory_space=pltpu.VMEM),
        out_shape=jax.ShapeDtypeStruct((8, 128), F32),
        compiler_params=pltpu.CompilerParams(vmem_limit_bytes=4 * MIB),
        cost_estimate=HEAVY,
        name="gate",
    )(*arrays)


def finish_kernel(me_ref, mine_ref, theirs_ref, *refs):
    gs_ref, gn_ref, gb_ref = refs[-3:]
    feat = gs_ref.shape[0]
    half = feat // 2
    core = me_ref[0] % 2
    for other, ref in ((0, mine_ref), (1, theirs_ref)):
        at = pl.ds(pl.multiple_of((core ^ other) * half, half), half)
        gs_ref[at] = ref[0:half]
        gn_ref[at] = ref[half:feat]
    gb_ref[...] = mine_ref[feat : feat + 1]


def finish(me, mine, theirs, after):
    vm = pl.BlockSpec(memory_space=pltpu.VMEM)
    rows, hidden = mine.shape
    feat = rows - 8
    return pl.pallas_call(
        finish_kernel,
        in_specs=[pl.BlockSpec(memory_space=pltpu.SMEM), vm, vm]
        + [pl.BlockSpec(memory_space=pl.ANY)] * len(after),
        out_specs=[vm] * 3,
        out_shape=[
            jax.ShapeDtypeStruct((feat, hidden), F32),
            jax.ShapeDtypeStruct((feat, hidden), F32),
            jax.ShapeDtypeStruct((1, hidden), F32),
        ],
        compiler_params=pltpu.CompilerParams(vmem_limit_bytes=4 * MIB),
        cost_estimate=LIGHT,
        name="finish",
    )(me, mine, theirs, *after)


def last_kernel(
    places, nb, n_arrays, marks, me_ref, mine_ref, theirs_ref, acc_ref, adj_hbm, *refs
):
    refs = refs[marks:]
    backs, out_ref, grads, scratch = refs[:n_arrays], refs[n_arrays], refs[-5:-2], refs[-2:]
    finish_kernel(me_ref, mine_ref, theirs_ref, *grads)
    spread_kernel(places, nb, n_arrays, 0, acc_ref, adj_hbm, *backs, out_ref, *scratch)


def spread(acc, adjacency, marks, places, backs, nb, dtype, heavy=True, grads=None):
    vm = pl.BlockSpec(memory_space=pltpu.VMEM)
    rows, feat = acc.shape
    per_unit = nb * nb
    tile = adjacency.shape[1]
    n = len(places)
    any_space = pl.BlockSpec(memory_space=pl.ANY)
    in_specs = [vm, any_space] + [any_space] * len(marks) + [vm] * len(backs)
    inputs = [acc, adjacency, *marks, *backs]
    kernel, out_shape = spread_kernel, jax.ShapeDtypeStruct((rows, feat), dtype)
    if grads is not None:
        in_specs = [pl.BlockSpec(memory_space=pltpu.SMEM), vm, vm] + in_specs
        inputs = [*grads, *inputs]
        hidden = grads[1].shape[1]
        kernel = last_kernel
        out_shape = [
            out_shape,
            jax.ShapeDtypeStruct((feat, hidden), F32),
            jax.ShapeDtypeStruct((feat, hidden), F32),
            jax.ShapeDtypeStruct((1, hidden), F32),
        ]
    return pl.pallas_call(
        functools.partial(kernel, tuple(places), nb, len(backs), len(marks)),
        in_specs=in_specs,
        out_specs=jax.tree.map(lambda _: vm, out_shape),
        out_shape=out_shape,
        scratch_shapes=[
            pltpu.VMEM((n, per_unit, tile, tile), BF16),
            pltpu.SemaphoreType.DMA((n,)),
        ],
        compiler_params=pltpu.CompilerParams(vmem_limit_bytes=12 * MIB),
        cost_estimate=HEAVY if heavy else LIGHT,
        name="spread",
    )(*inputs)


def tree_sum(values):
    while len(values) > 1:
        values = [values[i] + values[i + 1] for i in range(0, len(values), 2)]
    return values[0]


def stages_of(devices):
    bits = devices.bit_length() - 1
    assert 1 << bits == devices and bits >= 3
    rest = bits - 1
    return rest // 2, rest - rest // 2


def on_device(
    features,
    patterns,
    tile_dest,
    tile_src_block,
    tile_dst_block,
    in_degree,
    w_self,
    w_neigh,
    bias,
    cotangent,
):
    devices = lax.axis_size("row")
    me = lax.axis_index("row")
    tile = patterns.shape[1]
    rows, feat = features.shape
    nb = rows // tile
    y_bits, z_bits = stages_of(devices)
    ny, nz = 1 << y_bits, 1 << z_bits
    units = devices // 2
    small = devices == 16

    tiles_at = (tile_dest.reshape(-1), tile_src_block, tile_dst_block)

    parts = PLAN["halves"] if small else (tuple(range(min(GROUP, units))),)
    *s_other, s_own = forward_sums(
        devices, F32 if small else BF16, tiles_at, features, patterns, nb, parts
    )
    received = [swap(s, 1, devices) for s in s_other]
    s_recv = received[-1]
    from_other = {}
    for units_of, got in zip(parts, received, strict=True):
        if small:
            from_other.update({m: got[i] for i, m in enumerate(units_of)})
    if not small:
        from_other = {m: s_recv[m] for m in range(units)}

    def chip_sum(m):
        return s_own[m].astype(F32) + from_other[m].astype(F32)

    if small:
        y_recv = [None] * nz
        sent = None
        for n in PLAN["y"]:
            y_recv[n] = []
            if n in PLAN["direct"]:
                continue
            for k in range(1, ny):
                own, recv = s_own[n * ny + k], from_other[n * ny + k]
                if sent is not None and PLAN["ysep"]:
                    own, recv, sent = lax.optimization_barrier((own, recv, sent))
                sent = (own.astype(F32) + recv.astype(F32)).astype(BF16)
                y_recv[n].append(swap(sent, 2 * k, devices))
    else:
        s5 = s_own.reshape(nz, ny, feat, rows)
        r5 = s_recv.reshape(nz, ny, feat, rows)
        got = [
            swap((s5[:, k].astype(F32) + r5[:, k].astype(F32)).astype(BF16), 2 * k, devices)
            for k in range(1, ny)
        ]
        y_recv = [[g[n] for g in got] for n in range(nz)]
    z_recv = {}
    sent = None
    sums, first_sent, sent = {}, sent if small else None, None
    for n in PLAN["z"] if small else reversed(range(1, nz)):
        arrived = y_recv[n]
        if small and n in PLAN["direct"]:
            for k in range(ny):
                m = n * ny + k
                mine, recv, sent = s_own[m], from_other[m], first_sent
                if PLAN["dsep"]:
                    mine, recv, sent = lax.optimization_barrier((mine, recv, sent))
                direct = (mine.astype(F32) + recv.astype(F32)).astype(BF16)
                z_recv[m / ny] = swap(direct, 2 * m, devices)[None]
            continue
        if sent is not None:
            arrived, sent = lax.optimization_barrier((arrived, sent))
        total = chip_sum(n * ny)
        for r in arrived:
            total = total + r.astype(F32)
        sums[n] = sent = total.astype(BF16)
        z_recv[n] = swap(sent, 2 * ny * n, devices)[None]
    after = PLAN["after"] if small else 1
    made = s_recv
    if after == 4:
        adj, made = adjacency(devices, tiles_at, patterns, nb, z_recv[3])
    elif after:
        adj, made = adjacency(devices, tiles_at, patterns, nb, sums[after])
    total, summed = s_own, ()
    parts = PLAN["parts"] if small else [(n,) for n in range(2, nz)]
    for i, part in enumerate(parts):
        extra = [s_recv] if i == 0 else []
        total = add_first(total, extra + [z_recv[n] for n in part], made)
        summed += part
    if not parts:
        summed = ()
    rest = [z_recv[n] for n in z_recv if n not in summed]

    output, delta, aggt, back = layer(
        made,
        total,
        ([s_recv] if not parts else []) + [r[None] for r in y_recv[0]] + rest,
        in_degree.reshape(1, rows),
        features,
        cotangent,
        w_self,
        w_neigh,
        bias.reshape(1, -1),
    )
    if not after:
        adj, made = adjacency(devices, tiles_at, patterns, nb, back)
    me = me.reshape(1).astype(jnp.int32)
    scale = 1.0 / math.sqrt(rows * devices)
    terms, base = grad_terms(scale, me, features, delta, aggt, w_self)

    have = {0: back}
    for n in PLAN["agz"] if small else range(1, nz):
        have[n * ny] = swap(back, 2 * ny * n, devices)
    own = {0: back[None]}
    onward = []
    for n in range(nz):
        own[2 * n * ny] = have[n * ny][None]
        for k in range(1, ny):
            m = n * ny + k
            if small and n in PLAN["agd"]:
                own[2 * m] = swap(back, 2 * m, devices)[None]
            elif small and PLAN["yfs"] and n > 0:
                onward.append(n)
            else:
                own[2 * m] = swap(have[n * ny], 2 * k, devices)[None]
    if onward:
        key = tuple(2 * n * ny + 2 for n in onward)
        own[key] = swap(jnp.stack([have[n * ny] for n in onward]), 2, devices)

    def plus_one(key):
        return tuple(u + 1 for u in key) if isinstance(key, tuple) else (key + 1,)

    across = {}
    for keys in PLAN["pairs"] if small else [(key,) for key in own]:
        name = sum((plus_one(key) for key in keys), ())
        parts = [own[key] for key in keys]
        whole = jnp.concatenate(parts, axis=0) if len(parts) > 1 else parts[0]
        across[name] = swap(whole, 1, devices)

    def later(value, what):
        key = PLAN[what]
        if key is None or not small:
            return value
        value, own[key] = lax.optimization_barrier((value, own[key]))
        return value

    terms = later(terms, "terms")
    half = terms[0] + swap(terms[1], 1, devices)
    half = later(half, "gy")
    if PLAN["gyb"]:
        half = half.astype(BF16)
    half = tree_sum(
        [half.astype(F32)] + [swap(half, 2 * k, devices).astype(F32) for k in range(1, ny)]
    )
    half = later(half, "gz")
    y_half = half
    if PLAN["butter"] and small:
        for n in (1, 2):
            rounded = half.astype(BF16)
            half = rounded.astype(F32) + swap(rounded, 2 * ny * n, devices).astype(F32)
    else:
        rounded = half.astype(BF16)
        half = tree_sum(
            [rounded.astype(F32)]
            + [swap(rounded, 2 * ny * n, devices).astype(F32) for n in range(1, nz)]
        )
    second = swap(half, 1, devices)

    if small:
        groups, heavy = PLAN["groups"], PLAN["heavy"]
    else:
        singles = list(own) + list(across)
        groups = [singles[at : at + GROUP] for at in range(0, devices, GROUP)]
        heavy = [1] * len(groups)
    grad_feat = base
    for i, group in enumerate(groups):
        last = i == len(groups) - 1
        parts = [(u, own[u]) if u in own else (u, across[u]) for u in group]
        parts = [(u if isinstance(u, tuple) else (u,), b) for u, b in parts]
        places = [u for us, _ in parts for u in us]
        marks = []
        for at, keys, with_half in PLAN["gates"] if small else ():
            if at == i:
                marks.append(gate(*([grad_feat] if i else []), *[own[k] if k in own else across[k] for k in keys], *([y_half] if with_half else [])))
        grad_feat = spread(
            grad_feat,
            adj,
            marks,
            places,
            [b for _, b in parts],
            nb,
            BF16 if last else F32,
            heavy[i],
            (me, half, second) if last and PLAN["fin"] else None,
        )
    if PLAN["fin"]:
        grad_feat, grad_self, grad_neigh, grad_bias = grad_feat
    else:
        grad_self, grad_neigh, grad_bias = finish(me, half, second, [grad_feat] if PLAN["findep"] else [])
    return (output, grad_feat, grad_self, grad_neigh, grad_bias.reshape(-1))


def solution(mesh):
    return jax.shard_map(
        on_device,
        mesh=mesh,
        in_specs=(
            P(("grp", "row"), None),
            P(("grp", "row"), None, None),
            P(("grp", "row"), None),
            P(("grp", "row")),
            P(("grp", "row")),
            P(("grp", "row")),
            P(),
            P(),
            P(),
            P(("grp", "row"), None),
        ),
        out_specs=(
            P(("grp", "row"), None),
            P(("grp", "row"), None),
            P("grp", None),
            P("grp", None),
            P("grp"),
        ),
        check_vma=False,
    )
```
